32 devices in a mesh: sweep: 2 (over y), xsec: 16 (over z, x, core).
Axes of the slice: x: 2, y: 2, z: 4, core: 2. Of those that a mesh axis runs over, the one named last changes fastest.
Arguments:
- cond_block: bfloat16 [2, 16, 2, 24, 40, 128], P('sweep', 'xsec'), may hold values from -0.15625 to 0.15625
- interior_src: bfloat16 [2, 16, 2, 4, 40, 128], P('sweep', 'xsec'), may hold values from -6 to 6
- face_index: int32 [2, 16, 16, 192], P('sweep', 'xsec'), may hold values from 0 to 255
- owner_count: int32 [2, 16, 16], P('sweep', 'xsec'), may hold values from 1 to 8, as said below
- coupling: float32 [4, 2, 2048], P('sweep', None, 'xsec'), may hold values from -1 to 1
- schur_inv: bfloat16 [4, 2, 2048, 2048], P('sweep', None, None, 'xsec'), may hold values from -0.09375 to 0.09375
Outputs:
- sweep_sol: float32 [4, 8, 2048], P('sweep', None, 'xsec')
The draws below stay inside these ranges and needn't reach their ends.
Inputs may be any that keep to these rules, and one draw needn't show every extreme that they name: `owner_count`: every count is at least 1 and at most 8; in each sweep row some owner receives 8 live slots from every sender.
All inputs are finite; a program needn't handle non-finite values.
Results may differ from the reference program's by a relative error of at most 0.006.
Values may be sent and summed in bfloat16 or wider, within the bound.
No kernel may reach another device: no remote copies, remote signals or barrier semaphores. Data moves between devices by JAX's collectives and lax.ppermute only.
A program may use at most 64 MiB of HBM per device.

```python
import jax
import jax.numpy as jnp
from jax import lax

NT = 24
NI = 40
SRC = 4
LAY_DEV = 2
TR_DEV = 128
CAP = 8
LAYERS = 4
TRACE = 2048
ELEMS = 128
FACES = 192
SLOTS = 256
N_SWEEP = 2
N_XSEC = 16


def draw_owner_count(key, part):
    key_base, key_hot = jax.random.split(jax.random.fold_in(key, 17))
    base = jax.random.randint(key_base, (N_SWEEP, N_XSEC, N_XSEC), 1, CAP // 2 + 1)
    hottest = jax.random.randint(key_hot, (N_SWEEP, 1, 1), 0, N_XSEC)
    owners = jnp.arange(N_XSEC)[None, :, None]
    return jnp.where(owners == hottest, CAP, base).astype(jnp.int32)


def place_ends(array, key, smallest, top_value):
    longest = array.shape.index(max(array.shape))
    spots = []
    for shift in (0, 1):
        where = [jax.random.randint(jax.random.fold_in(key, axis), (), 0, length) for axis, length in enumerate(array.shape)]
        where[longest] = (where[longest] + shift) % array.shape[longest]
        spots.append(tuple(where))
    return array.at[spots[0]].set(smallest).at[spots[1]].set(top_value)


def levels(rng, dims, shards, least, largest):
    def one(dim, parts):
        draws = jax.random.uniform(jax.random.fold_in(jax.random.fold_in(rng, 6), dim), (parts,), jnp.float32, least / len(shards), largest / len(shards))
        return jnp.repeat(jnp.exp(draws), dims[dim] // parts).reshape((-1,) + (1,) * (len(dims) - dim - 1))

    gain = one(*shards[0])
    for cut in shards[1:]:
        gain = gain * one(*cut)
    return gain


def noise(stream_key, shape, scale, limit, cuts=(), kind=jnp.bfloat16):
    drawn = scale * jax.random.normal(stream_key, shape, jnp.float32)
    if cuts:
        drawn = drawn * levels(stream_key, shape, cuts, -0.22, 0.18)
    return jnp.clip(drawn, -limit, limit).astype(kind)


def setup_inputs(seed: int = 0) -> dict:
    key_list = jax.random.split(jax.random.key(seed), 7)
    return {
        "cond_block": noise(key_list[0], (N_SWEEP, N_XSEC, 2, NT, NI, ELEMS), (32 * NI) ** -0.5, 0.15625, ((0, 2), (1, 16))),
        "interior_src": noise(key_list[1], (N_SWEEP, N_XSEC, 2, SRC, NI, ELEMS), 1.0, 6.0, ((0, 2), (1, 16))),
        "face_index": place_ends(jax.random.randint(key_list[2], (N_SWEEP, N_XSEC, N_XSEC, FACES), 0, SLOTS), jax.random.fold_in(key_list[2], 1), 0, SLOTS - 1).astype(jnp.int32),
        "owner_count": draw_owner_count(jax.random.fold_in(key_list[6], 71), 0),
        "coupling": jnp.clip(jax.random.uniform(key_list[4], (LAYERS, 2, TRACE), jnp.float32, -1.0, 1.0) * levels(key_list[4], (LAYERS, 2, TRACE), ((0, 2), (2, 16)), -0.4, 0.0), -1.0, 1.0),
        "schur_inv": noise(key_list[5], (LAYERS, 2, TRACE, TRACE), (2 * TRACE) ** -0.5, 0.09375, ((0, 2), (3, 16))),
    }


def condense(blocks, interior):
    left = blocks.astype(jnp.float32).reshape(N_XSEC, 2, NT, NI, N_XSEC, CAP)
    right = interior.astype(jnp.float32).reshape(N_XSEC, 2, SRC, NI, N_XSEC, CAP)

    def contract(first, second):
        return jnp.einsum("ckidp,csidp->dcskp", first, second, precision=lax.Precision.HIGHEST)

    real_part = contract(left[:, 0], right[:, 0]) - contract(left[:, 1], right[:, 1])
    imag_part = contract(left[:, 0], right[:, 1]) + contract(left[:, 1], right[:, 0])
    return jnp.stack([real_part, imag_part], 2).reshape(N_XSEC, N_XSEC, 2 * SRC, FACES)


def assemble_row(packed):
    blocks, interior, index_row, count_row = packed
    values = condense(blocks, interior)
    positions = (jnp.arange(FACES) % CAP).astype(jnp.int32)
    live_mask = positions[None, None, :] < count_row[:, :, None]
    values = jnp.where(live_mask[:, :, None, :], values, jnp.float32(0.0))
    owners = (jnp.arange(N_XSEC) * SLOTS).astype(jnp.int32)
    seg_ids = (index_row + owners[:, None, None]).astype(jnp.int32)
    flat_values = jnp.moveaxis(values, 2, 3).reshape(-1, 2 * SRC)
    summed = jax.ops.segment_sum(flat_values, seg_ids.reshape(-1), num_segments=N_XSEC * SLOTS)
    summed = summed.reshape(N_XSEC, LAY_DEV, TR_DEV, 2 * SRC)
    return summed.transpose(1, 3, 0, 2).reshape(LAY_DEV, 2 * SRC, TRACE)


def reference(cond_block, interior_src, face_index, owner_count, coupling, schur_inv):
    loads = lax.map(assemble_row, (cond_block, interior_src, face_index, owner_count))
    loads = loads.reshape(LAYERS, 2 * SRC, TRACE)
    carried = jnp.zeros((2, SRC, TRACE), jnp.float32)
    outputs = []
    for layer_at in range(LAYERS):
        layer_loads = loads[layer_at].reshape(2, SRC, TRACE)
        couple = coupling[layer_at]
        real_part = layer_loads[0] - (couple[0] * carried[0] - couple[1] * carried[1])
        imag_part = layer_loads[1] - (couple[0] * carried[1] + couple[1] * carried[0])
        rhs = jnp.concatenate([real_part, imag_part], 0).astype(jnp.bfloat16)
        first = jnp.dot(rhs, schur_inv[layer_at, 0], preferred_element_type=jnp.float32)
        second = jnp.dot(rhs, schur_inv[layer_at, 1], preferred_element_type=jnp.float32)
        carried = jnp.stack([first[:SRC] - second[SRC:], second[:SRC] + first[SRC:]], 0)
        outputs.append(carried.reshape(2 * SRC, TRACE))
    return jnp.stack(outputs, 0)
```

```python
import jax
import jax.numpy as jnp
from jax import lax
from jax.sharding import PartitionSpec as P

CAP = 8


def spread(block, axes, count):
    copies = jnp.broadcast_to(block[None], (count,) + block.shape)
    return lax.all_to_all(copies, axes, split_axis=0, concat_axis=0, tiled=True)


def widen(gathered):
    return jnp.moveaxis(gathered, 0, 1).reshape(gathered.shape[1], -1)


def couple(loads, coupling_layer, carried):
    real_part = loads[0] - (coupling_layer[0] * carried[0] - coupling_layer[1] * carried[1])
    imag_part = loads[1] - (coupling_layer[0] * carried[1] + coupling_layer[1] * carried[0])
    return jnp.concatenate([real_part, imag_part], 0).astype(jnp.bfloat16)


def apply_schur(rhs, schur_layer):
    count = rhs.shape[0] // 2
    first = jnp.dot(rhs, schur_layer[0], preferred_element_type=jnp.float32)
    second = jnp.dot(rhs, schur_layer[1], preferred_element_type=jnp.float32)
    return jnp.stack([first[:count] - second[count:], second[:count] + first[count:]], 0)


def shards(cond_block, interior_src, face_index, owner_count, coupling, schur_inv):
    layers_here = schur_inv.shape[0]
    width = schur_inv.shape[3]
    sources = interior_src.shape[3]
    n_faces = cond_block.shape[3]
    n_inner = cond_block.shape[4]
    peers = lax.axis_size("xsec")
    chain = lax.axis_size("sweep")
    face_rows_len = n_faces * CAP
    couple_blocks = cond_block[0, 0].reshape(2, n_faces, n_inner, peers, CAP)
    interior = interior_src[0, 0].reshape(2, sources, n_inner, peers, CAP)

    def contract(first, second):
        return jnp.einsum("kidp,sidp->dskp", first, second, preferred_element_type=jnp.float32)

    real_part = contract(couple_blocks[0], interior[0]) - contract(couple_blocks[1], interior[1])
    imag_part = contract(couple_blocks[0], interior[1]) + contract(couple_blocks[1], interior[0])
    outgoing_rows = jnp.stack([real_part, imag_part], 1).reshape(peers, 2 * sources, face_rows_len)
    outgoing_rows = outgoing_rows.astype(jnp.bfloat16)
    index_rows = face_index[0, 0]
    positions = jnp.arange(face_rows_len) % CAP
    live_mask = positions[None, :] < owner_count[0, 0][:, None]
    slot_ids = jnp.arange(layers_here * width)
    received = lax.all_to_all(outgoing_rows, "xsec", split_axis=0, concat_axis=0, tiled=True)

    onehot = jnp.where(
        (index_rows[:, :, None] == slot_ids[None, None, :]) & live_mask[:, :, None], 1.0, 0.0
    ).astype(jnp.bfloat16)
    assembled = jnp.einsum("cmf,cfz->mz", received, onehot, preferred_element_type=jnp.float32)
    loads_all = assembled.reshape(2, sources, layers_here, width)

    coupling_high = coupling[0].astype(jnp.bfloat16)
    coupling_low = (coupling[0] - coupling_high.astype(jnp.float32)).astype(jnp.bfloat16)
    first_loads = loads_all[:, :, 0].reshape(2 * sources, width).astype(jnp.bfloat16)
    rows = jnp.concatenate([first_loads, coupling_high, coupling_low], 0)
    pad = -rows.shape[0] % 16
    rows = jnp.concatenate([rows, jnp.zeros((pad, width), jnp.bfloat16)], 0)
    whole = widen(spread(rows, "xsec", peers))
    full_loads = whole[: 2 * sources].astype(jnp.float32).reshape(2, sources, -1)
    full_coupling = (
        whole[2 * sources : 2 * sources + 2].astype(jnp.float32)
        + whole[2 * sources + 2 : 2 * sources + 4].astype(jnp.float32)
    )
    row_at = lax.axis_index("sweep")
    before = jnp.zeros((2, sources, peers * width), jnp.float32)
    for round_at in range(chain):
        if round_at:
            everyone = spread(carried.reshape(2 * sources, width).astype(jnp.bfloat16), ("sweep", "xsec"), chain * peers)
            start = jnp.maximum(row_at - 1, 0) * peers
            previous = widen(lax.dynamic_slice_in_dim(everyone, start, peers, 0)).astype(jnp.float32)
            previous = jnp.where(row_at > 0, previous, 0.0)
            before = previous.reshape(2, sources, peers * width)
        carried = apply_schur(couple(full_loads, full_coupling, before), schur_inv[0])
        layers_out = [carried]
        for layer_at in range(1, layers_here):
            rhs = couple(loads_all[:, :, layer_at], coupling[layer_at], carried)
            carried = apply_schur(widen(spread(rhs, "xsec", peers)), schur_inv[layer_at])
            layers_out.append(carried)
    solved = jnp.stack(layers_out, 0)
    return solved.reshape(layers_here, 2 * sources, width)


def solution(mesh):
    placed = (
        P("sweep", "xsec", None, None, None, None),
        P("sweep", "xsec", None, None, None, None),
        P("sweep", "xsec", None, None),
        P("sweep", "xsec", None),
        P("sweep", None, "xsec"),
        P("sweep", None, None, "xsec"),
    )
    return jax.shard_map(
        shards, mesh=mesh, in_specs=placed, out_specs=P("sweep", None, "xsec"), check_vma=False
    )
```

```python
import functools

import jax
import jax.numpy as jnp
from jax import lax
from jax.experimental import pallas as pl
from jax.experimental.pallas import tpu as pltpu
from jax.sharding import PartitionSpec as P

CAP = 8
LANES = 128
F32 = jnp.float32
BF16 = jnp.bfloat16


def iota(shape, axis):
    return lax.broadcasted_iota(jnp.int32, shape, axis)


def sum_sublanes(tiles):
    sub = iota((8, LANES), 0)
    low = sub < 4
    halves = [
        jnp.where(low, tiles[r], tiles[r + 4]) + pltpu.roll(jnp.where(low, tiles[r + 4], tiles[r]), 4, 0)
        for r in range(4)
    ]

    def fold(first, second, step):
        even = (sub & step) == 0
        return jnp.where(even, first, second) + jnp.where(
            even, pltpu.roll(first, 8 - step, 0), pltpu.roll(second, step, 0)
        )

    pairs = [fold(halves[r], halves[r + 2], 2) for r in range(2)]
    return fold(pairs[0], pairs[1], 1)


def swap_blocks(tiles, group):
    lane = iota((8, LANES), 1) // group
    tiles = list(tiles)
    bit = len(tiles) // 2
    while bit:
        here = (lane & bit) == 0
        for at in range(len(tiles)):
            if at & bit == 0:
                low, high = tiles[at], tiles[at + bit]
                tiles[at] = jnp.where(here, low, pltpu.roll(high, bit * group, 1))
                tiles[at + bit] = jnp.where(here, pltpu.roll(low, LANES - bit * group, 1), high)
        bit //= 2
    return tiles


def contract_kernel(cond, source, out, source32, rows):
    _, n_faces, n_inner, elems = cond.shape
    sources = source.shape[1]
    owners = LANES // CAP
    for block in range(elems // LANES):
        lanes = pl.ds(block * LANES, LANES)
        source32[...] = source[:, :, :, lanes].astype(F32)

        def one_face(face, _):
            left_re = cond[0, face, :, lanes].astype(F32)
            left_im = cond[1, face, :, lanes].astype(F32)
            tiles = [None] * (2 * sources)
            for j in range(sources):
                right_re, right_im = source32[0, j], source32[1, j]
                real = left_re * right_re - left_im * right_im
                imag = left_re * right_im + left_im * right_re
                tiles[j] = jnp.sum(real.reshape(n_inner // 8, 8, LANES), 0)
                tiles[sources + j] = jnp.sum(imag.reshape(n_inner // 8, 8, LANES), 0)
            rows[face] = sum_sublanes(tiles)
            return 0

        lax.fori_loop(0, n_faces, one_face, 0, unroll=True)
        parts = [[] for _ in range(owners)]
        at = 0
        while at < n_faces:
            size = owners
            while size > n_faces - at:
                size //= 2
            moved = swap_blocks([rows[at + face] for face in range(size)], CAP)
            for owner in range(owners):
                piece = moved[owner % size]
                skip = owner // size * size * CAP
                if skip:
                    piece = pltpu.roll(piece, LANES - skip, 1)
                parts[owner].append(piece[:, : size * CAP])
            at += size
        for owner in range(owners):
            out[block * owners + owner] = jnp.concatenate(parts[owner], 1).astype(BF16)


def assemble_kernel(received, index_rows, counts, coupling, loads, out):
    peers, rows, face_rows = received.shape
    slots = loads.shape[0] * loads.shape[2]
    width = loads.shape[2]
    position = iota((1, face_rows), 1) % CAP
    slot = iota((slots, face_rows), 0)
    total = jnp.zeros((rows, slots), F32)
    for sender in range(peers):
        index = jnp.where(position < counts[sender], index_rows[sender : sender + 1, :], -1)
        onehot = jnp.where(slot == index, 1.0, 0.0).astype(BF16)
        total += lax.dot_general(
            received[sender], onehot, (((1,), (1,)), ((), ())), preferred_element_type=F32
        )
    for layer in range(loads.shape[0]):
        loads[layer] = total[:, layer * width : (layer + 1) * width]
    couple_first = coupling[0]
    high = couple_first.astype(BF16).astype(F32)
    extra = jnp.concatenate([high, couple_first - high, jnp.zeros((4, width), F32)], 0)
    block = jnp.concatenate([total[:, :width], extra], 0).astype(BF16)
    for peer in range(out.shape[0]):
        out[peer] = block


def side_by_side(blocks):
    return jnp.concatenate(blocks, 1)


def couple(loads, coupling, carried):
    half = loads.shape[0] // 2
    couple_re, couple_im = coupling[0:1], coupling[1:2]
    real, imag = carried[:half], carried[half:]
    return jnp.concatenate(
        [
            loads[:half] - (couple_re * real - couple_im * imag),
            loads[half:] - (couple_re * imag + couple_im * real),
        ],
        0,
    )


def apply_schur(rhs, schur, layer):
    half = rhs.shape[0] // 2
    first = jnp.dot(rhs, schur[layer, 0], preferred_element_type=F32)
    second = jnp.dot(rhs, schur[layer, 1], preferred_element_type=F32)
    return jnp.concatenate([first[:half] - second[half:], second[:half] + first[half:]], 0)


def start_kernel(whole, loads, coupling, schur, out):
    count = loads.shape[1]
    rhs = side_by_side([whole[peer].astype(F32)[:count].astype(BF16) for peer in range(whole.shape[0])])
    solved = apply_schur(rhs, schur, 0)
    block = couple(loads[1], coupling[1], solved).astype(BF16)
    for peer in range(out.shape[0]):
        out[peer] = block


def next_kernel(gathered, loads, coupling, schur, out, *, layer):
    solved = apply_schur(side_by_side([gathered[peer] for peer in range(gathered.shape[0])]), schur, layer)
    block = solved.astype(BF16) if loads is None else couple(loads[layer + 1], coupling[layer + 1], solved).astype(BF16)
    for peer in range(out.shape[0]):
        out[peer] = block


def cross_kernel(everyone, whole, loads, coupling, schur, out, solved_out):
    peers = whole.shape[0]
    count = loads.shape[1]
    row = lax.axis_index("sweep")
    start = jnp.maximum(row - 1, 0) * peers
    keep = (row > 0).astype(F32)
    blocks = []
    for peer in range(peers):
        piece = whole[peer].astype(F32)
        pair = piece[count : count + 2] + piece[count + 2 : count + 4]
        before = everyone[start + peer].astype(F32) * keep
        blocks.append(couple(piece[:count], pair, before).astype(BF16))
    solved = apply_schur(side_by_side(blocks), schur, 0)
    solved_out[...] = solved
    block = couple(loads[1], coupling[1], solved).astype(BF16)
    for peer in range(out.shape[0]):
        out[peer] = block


def last_kernel(gathered, first, schur, out, *, layer):
    out[0] = first[...]
    out[layer] = apply_schur(
        side_by_side([gathered[peer] for peer in range(gathered.shape[0])]), schur, layer
    )


def call(kernel, out_shape, operands, scratch=(), scalars=()):
    specs = [
        pl.BlockSpec(memory_space=pltpu.SMEM if at in scalars else pltpu.VMEM) for at in range(len(operands))
    ]
    out_specs = jax.tree.map(lambda _: pl.BlockSpec(memory_space=pltpu.VMEM), out_shape)
    return pl.pallas_call(
        kernel,
        out_shape=out_shape,
        in_specs=specs,
        out_specs=out_specs,
        scratch_shapes=list(scratch),
        compiler_params=pltpu.CompilerParams(vmem_limit_bytes=16 * 1024 * 1024),
    )(*operands)


def exchange(blocks, axes):
    return lax.all_to_all(blocks, axes, split_axis=0, concat_axis=0, tiled=True)


def shards(cond_block, interior_src, face_index, owner_count, coupling, schur_inv):
    layers = schur_inv.shape[0]
    width = schur_inv.shape[3]
    sources = interior_src.shape[3]
    n_faces, n_inner, elems = cond_block.shape[3:]
    peers = lax.axis_size("xsec")
    chain = lax.axis_size("sweep")
    count = 2 * sources
    struct = jax.ShapeDtypeStruct

    outgoing = call(
        contract_kernel,
        struct((peers, count, n_faces * CAP), BF16),
        (cond_block[0, 0], interior_src[0, 0]),
        scratch=(pltpu.VMEM((2, sources, n_inner, LANES), F32), pltpu.VMEM((n_faces, count, LANES), F32)),
    )
    received = exchange(outgoing, "xsec")
    loads, block = call(
        assemble_kernel,
        (struct((layers, count, width), F32), struct((peers, 16, width), BF16)),
        (received, face_index[0, 0], owner_count[0, 0], coupling),
        scalars=(2,),
    )
    whole = exchange(block, "xsec")
    gathered_shape = struct((peers, count, width), BF16)
    block = call(start_kernel, gathered_shape, (whole, loads, coupling, schur_inv))
    for round_at in range(chain):
        if round_at:
            block, first = call(
                cross_kernel,
                (gathered_shape, struct((count, width), F32)),
                (everyone, whole, loads, coupling, schur_inv),
            )
        for layer in range(1, layers - 1):
            raise NotImplementedError
        gathered = exchange(block, "xsec")
        if round_at < chain - 1:
            block = call(
                functools.partial(send_kernel, layer=layers - 1),
                struct((chain * peers, count, width), BF16),
                (gathered, schur_inv),
            )
            everyone = exchange(block, ("sweep", "xsec"))
    return call(
        functools.partial(last_kernel, layer=layers - 1),
        struct((layers, count, width), F32),
        (gathered, first, schur_inv),
    )


def send_kernel(gathered, schur, out, *, layer):
    next_kernel(gathered, None, None, schur, out, layer=layer)


def solution(mesh):
    placed = (
        P("sweep", "xsec", None, None, None, None),
        P("sweep", "xsec", None, None, None, None),
        P("sweep", "xsec", None, None),
        P("sweep", "xsec", None),
        P("sweep", None, "xsec"),
        P("sweep", None, None, "xsec"),
    )
    return jax.shard_map(
        shards, mesh=mesh, in_specs=placed, out_specs=P("sweep", None, "xsec"), check_vma=False
    )
```

```python
import functools

import jax
import jax.numpy as jnp
from jax import lax
from jax.experimental import pallas as pl
from jax.experimental.pallas import tpu as pltpu
from jax.sharding import PartitionSpec as P

CAP = 8
LANES = 128
CHUNKS = 4
F32 = jnp.float32
BF16 = jnp.bfloat16


def iota(shape, axis):
    return lax.broadcasted_iota(jnp.int32, shape, axis)


def sum_sublanes(tiles):
    sub = iota((8, LANES), 0)
    low = sub < 4
    halves = [
        jnp.where(low, tiles[r], tiles[r + 4]) + pltpu.roll(jnp.where(low, tiles[r + 4], tiles[r]), 4, 0)
        for r in range(4)
    ]

    def fold(first, second, step):
        even = (sub & step) == 0
        return jnp.where(even, first, second) + jnp.where(
            even, pltpu.roll(first, 8 - step, 0), pltpu.roll(second, step, 0)
        )

    pairs = [fold(halves[r], halves[r + 2], 2) for r in range(2)]
    return fold(pairs[0], pairs[1], 1)


def swap_blocks(tiles, group):
    lane = iota((8, LANES), 1) // group
    tiles = list(tiles)
    bit = len(tiles) // 2
    while bit:
        here = (lane & bit) == 0
        for at in range(len(tiles)):
            if at & bit == 0:
                low, high = tiles[at], tiles[at + bit]
                tiles[at] = jnp.where(here, low, pltpu.roll(high, bit * group, 1))
                tiles[at + bit] = jnp.where(here, pltpu.roll(low, LANES - bit * group, 1), high)
        bit //= 2
    return tiles


def contract_kernel(
    cond_hbm, source_hbm, index_hbm, counts_hbm, coupling_hbm, schur_hbm,
    out, index_out, coupling_out, schur_out,
    cond, source, index_rows, counts, source32, rows, sems,
):
    _, n_faces, n_inner, elems = cond.shape
    sources = source.shape[1]
    owners = LANES // CAP
    faces_each = n_faces // CHUNKS
    copies = [pltpu.make_async_copy(source_hbm, source, sems.at[0])]
    for chunk in range(CHUNKS):
        some = pl.ds(chunk * faces_each, faces_each)
        copies.append(pltpu.make_async_copy(cond_hbm.at[:, some], cond.at[:, some], sems.at[1 + chunk]))
    rest = [
        pltpu.make_async_copy(index_hbm, index_rows, sems.at[1 + CHUNKS]),
        pltpu.make_async_copy(counts_hbm, counts, sems.at[2 + CHUNKS]),
        pltpu.make_async_copy(coupling_hbm, coupling_out, sems.at[3 + CHUNKS]),
        pltpu.make_async_copy(schur_hbm, schur_out, sems.at[4 + CHUNKS]),
    ]
    for copy in copies + rest:
        copy.start()
    copies[0].wait()
    for block in range(elems // LANES):
        lanes = pl.ds(block * LANES, LANES)
        source32[:2] = source[:, :, :, lanes].astype(F32)
        source32[2] = source32[0] + source32[1]
        for face in range(n_faces):
            if block == 0 and face % faces_each == 0:
                copies[1 + face // faces_each].wait()
            left_re = cond[0, face, :, lanes].astype(F32)
            left_im = cond[1, face, :, lanes].astype(F32)
            left_sum = left_re + left_im
            left_gap = left_im - left_re
            tiles = [None] * (2 * sources)
            for j in range(sources):
                both = jnp.sum((left_re * source32[2, j]).reshape(n_inner // 8, 8, LANES), 0)
                minus = jnp.sum((left_sum * source32[1, j]).reshape(n_inner // 8, 8, LANES), 0)
                plus = jnp.sum((left_gap * source32[0, j]).reshape(n_inner // 8, 8, LANES), 0)
                tiles[j] = both - minus
                tiles[sources + j] = both + plus
            rows[face] = sum_sublanes(tiles)
        parts = [[] for _ in range(owners)]
        at = 0
        while at < n_faces:
            size = owners
            while size > n_faces - at:
                size //= 2
            moved = swap_blocks([rows[at + face] for face in range(size)], CAP)
            for owner in range(owners):
                piece = moved[owner % size]
                skip = owner // size * size * CAP
                if skip:
                    piece = pltpu.roll(piece, LANES - skip, 1)
                parts[owner].append(piece[:, : size * CAP])
            at += size
        for owner in range(owners):
            out[block * owners + owner] = jnp.concatenate(parts[owner], 1).astype(BF16)
    for copy in rest:
        copy.wait()
    position = iota((1, index_rows.shape[1]), 1) % CAP
    for sender in range(index_rows.shape[0]):
        row = index_rows[sender : sender + 1, :]
        index_out[sender : sender + 1, :] = jnp.where(position < counts[sender], row, -1)


def assemble_kernel(received, index_rows, coupling, loads, out):
    peers, rows, face_rows = received.shape
    slots = loads.shape[0] * loads.shape[2]
    width = loads.shape[2]
    slot = iota((slots, face_rows), 0)
    total = jnp.zeros((rows, slots), F32)
    for sender in range(peers):
        onehot = jnp.where(slot == index_rows[sender : sender + 1, :], 1.0, 0.0).astype(BF16)
        total += lax.dot_general(
            received[sender], onehot, (((1,), (1,)), ((), ())), preferred_element_type=F32
        )
    for layer in range(loads.shape[0]):
        loads[layer] = total[:, layer * width : (layer + 1) * width]
    couple_first = coupling[0]
    high = couple_first.astype(BF16).astype(F32)
    extra = jnp.concatenate([high, couple_first - high, jnp.zeros((4, width), F32)], 0)
    block = jnp.concatenate([total[:, :width], extra], 0).astype(BF16)
    for peer in range(out.shape[0]):
        out[peer] = block


def side_by_side(blocks):
    return jnp.concatenate(blocks, 1)


def couple(loads, coupling, carried):
    half = loads.shape[0] // 2
    couple_re, couple_im = coupling[0:1], coupling[1:2]
    real, imag = carried[:half], carried[half:]
    return jnp.concatenate(
        [
            loads[:half] - (couple_re * real - couple_im * imag),
            loads[half:] - (couple_re * imag + couple_im * real),
        ],
        0,
    )


def apply_schur(rhs, schur, layer):
    half = rhs.shape[0] // 2
    first = jnp.dot(rhs, schur[layer, 0], preferred_element_type=F32)
    second = jnp.dot(rhs, schur[layer, 1], preferred_element_type=F32)
    return jnp.concatenate([first[:half] - second[half:], second[:half] + first[half:]], 0)


def start_kernel(whole, loads, coupling, schur, out):
    count = loads.shape[1]
    rhs = side_by_side([whole[peer].astype(F32)[:count].astype(BF16) for peer in range(whole.shape[0])])
    solved = apply_schur(rhs, schur, 0)
    block = couple(loads[1], coupling[1], solved).astype(BF16)
    for peer in range(out.shape[0]):
        out[peer] = block


def next_kernel(gathered, loads, coupling, schur, out, *, layer):
    solved = apply_schur(side_by_side([gathered[peer] for peer in range(gathered.shape[0])]), schur, layer)
    block = solved.astype(BF16) if loads is None else couple(loads[layer + 1], coupling[layer + 1], solved).astype(BF16)
    for peer in range(out.shape[0]):
        out[peer] = block


def cross_kernel(everyone, whole, loads, coupling, schur, out, solved_out):
    peers = whole.shape[0]
    count = loads.shape[1]
    row = lax.axis_index("sweep")
    start = jnp.maximum(row - 1, 0) * peers
    keep = (row > 0).astype(F32)
    blocks = []
    for peer in range(peers):
        piece = whole[peer].astype(F32)
        pair = piece[count : count + 2] + piece[count + 2 : count + 4]
        before = everyone[start + peer].astype(F32) * keep
        blocks.append(couple(piece[:count], pair, before).astype(BF16))
    solved = apply_schur(side_by_side(blocks), schur, 0)
    solved_out[...] = solved
    block = couple(loads[1], coupling[1], solved).astype(BF16)
    for peer in range(out.shape[0]):
        out[peer] = block


def last_kernel(gathered, first, schur, out, *, layer):
    out[0] = first[...]
    out[layer] = apply_schur(
        side_by_side([gathered[peer] for peer in range(gathered.shape[0])]), schur, layer
    )


def call(kernel, out_shape, operands, scratch=(), space=pltpu.VMEM):
    if space == pltpu.HBM:
        operands = [pltpu.with_memory_space_constraint(operand, space) for operand in operands]
    return pl.pallas_call(
        kernel,
        out_shape=out_shape,
        in_specs=[pl.BlockSpec(memory_space=space)] * len(operands),
        out_specs=jax.tree.map(lambda _: pl.BlockSpec(memory_space=pltpu.VMEM), out_shape),
        scratch_shapes=list(scratch),
        compiler_params=pltpu.CompilerParams(vmem_limit_bytes=16 * 1024 * 1024),
    )(*operands)


def exchange(blocks, axes):
    return lax.all_to_all(blocks, axes, split_axis=0, concat_axis=0, tiled=True)


def shards(cond_block, interior_src, face_index, owner_count, coupling, schur_inv):
    layers = schur_inv.shape[0]
    width = schur_inv.shape[3]
    sources = interior_src.shape[3]
    n_faces, n_inner, elems = cond_block.shape[3:]
    peers = lax.axis_size("xsec")
    chain = lax.axis_size("sweep")
    count = 2 * sources
    struct = jax.ShapeDtypeStruct

    index_rows = face_index[0, 0]
    outgoing, index_rows, coupling, schur_inv = call(
        contract_kernel,
        (
            struct((peers, count, n_faces * CAP), BF16),
            struct(index_rows.shape, index_rows.dtype),
            struct(coupling.shape, coupling.dtype),
            struct(schur_inv.shape, schur_inv.dtype),
        ),
        (cond_block[0, 0], interior_src[0, 0], index_rows, owner_count[0, 0], coupling, schur_inv),
        scratch=(
            pltpu.VMEM(cond_block.shape[2:], BF16),
            pltpu.VMEM(interior_src.shape[2:], BF16),
            pltpu.VMEM(index_rows.shape, index_rows.dtype),
            pltpu.SMEM(owner_count.shape[2:], owner_count.dtype),
            pltpu.VMEM((3, sources, n_inner, LANES), F32),
            pltpu.VMEM((n_faces, count, LANES), F32),
            pltpu.SemaphoreType.DMA((5 + CHUNKS,)),
        ),
        space=pltpu.HBM,
    )
    received = exchange(outgoing, "xsec")
    loads, block = call(
        assemble_kernel,
        (struct((layers, count, width), F32), struct((peers, 16, width), BF16)),
        (received, index_rows, coupling),
    )
    whole = exchange(block, "xsec")
    gathered_shape = struct((peers, count, width), BF16)
    block = call(start_kernel, gathered_shape, (whole, loads, coupling, schur_inv))
    for round_at in range(chain):
        if round_at:
            block, first = call(
                cross_kernel,
                (gathered_shape, struct((count, width), F32)),
                (everyone, whole, loads, coupling, schur_inv),
            )
        for layer in range(1, layers - 1):
            raise NotImplementedError
        gathered = exchange(block, "xsec")
        if round_at < chain - 1:
            block = call(
                functools.partial(send_kernel, layer=layers - 1),
                struct((chain * peers, count, width), BF16),
                (gathered, schur_inv),
            )
            everyone = exchange(block, ("sweep", "xsec"))
    return call(
        functools.partial(last_kernel, layer=layers - 1),
        struct((layers, count, width), F32),
        (gathered, first, schur_inv),
    )


def send_kernel(gathered, schur, out, *, layer):
    next_kernel(gathered, None, None, schur, out, layer=layer)


def solution(mesh):
    placed = (
        P("sweep", "xsec", None, None, None, None),
        P("sweep", "xsec", None, None, None, None),
        P("sweep", "xsec", None, None),
        P("sweep", "xsec", None),
        P("sweep", None, "xsec"),
        P("sweep", None, None, "xsec"),
    )
    return jax.shard_map(
        shards, mesh=mesh, in_specs=placed, out_specs=P("sweep", None, "xsec"), check_vma=False
    )
```

```python
import functools

import jax
import jax.numpy as jnp
from jax import lax
from jax.experimental import pallas as pl
from jax.experimental.pallas import tpu as pltpu
from jax.sharding import PartitionSpec as P

CAP = 8
LANES = 128
CHUNKS = 4
F32 = jnp.float32
BF16 = jnp.bfloat16


def iota(shape, axis):
    return lax.broadcasted_iota(jnp.int32, shape, axis)


def sum_sublanes(tiles):
    sub = iota((8, LANES), 0)
    low = sub < 4
    halves = [
        jnp.where(low, tiles[r], tiles[r + 4]) + pltpu.roll(jnp.where(low, tiles[r + 4], tiles[r]), 4, 0)
        for r in range(4)
    ]

    def fold(first, second, step):
        even = (sub & step) == 0
        return jnp.where(even, first, second) + jnp.where(
            even, pltpu.roll(first, 8 - step, 0), pltpu.roll(second, step, 0)
        )

    pairs = [fold(halves[r], halves[r + 2], 2) for r in range(2)]
    return fold(pairs[0], pairs[1], 1)


def swap_blocks(tiles, group):
    lane = iota((8, LANES), 1) // group
    tiles = list(tiles)
    bit = len(tiles) // 2
    while bit:
        here = (lane & bit) == 0
        for at in range(len(tiles)):
            if at & bit == 0:
                low, high = tiles[at], tiles[at + bit]
                tiles[at] = jnp.where(here, low, pltpu.roll(high, bit * group, 1))
                tiles[at + bit] = jnp.where(here, pltpu.roll(low, LANES - bit * group, 1), high)
        bit //= 2
    return tiles


def contract_kernel(
    cond_hbm, source_hbm, index_hbm, counts_hbm, coupling_hbm, schur_hbm,
    out, index_out, coupling_out, schur_out,
    cond, source, index_rows, counts, source32, rows, sems,
):
    _, n_faces, n_inner, elems = cond.shape
    sources = source.shape[1]
    owners = LANES // CAP
    faces_each = n_faces // CHUNKS
    copies = [pltpu.make_async_copy(source_hbm, source, sems.at[0])]
    for chunk in range(CHUNKS):
        some = pl.ds(chunk * faces_each, faces_each)
        copies.append(pltpu.make_async_copy(cond_hbm.at[:, some], cond.at[:, some], sems.at[1 + chunk]))
    rest = [
        pltpu.make_async_copy(index_hbm, index_rows, sems.at[1 + CHUNKS]),
        pltpu.make_async_copy(counts_hbm, counts, sems.at[2 + CHUNKS]),
        pltpu.make_async_copy(coupling_hbm, coupling_out, sems.at[3 + CHUNKS]),
        pltpu.make_async_copy(schur_hbm, schur_out, sems.at[4 + CHUNKS]),
    ]
    for copy in copies + rest:
        copy.start()
    copies[0].wait()
    for block in range(elems // LANES):
        lanes = pl.ds(block * LANES, LANES)
        source32[:2] = source[:, :, :, lanes].astype(F32)
        source32[2] = source32[0] + source32[1]
        for face in range(n_faces):
            if block == 0 and face % faces_each == 0:
                copies[1 + face // faces_each].wait()
            left_re = cond[0, face, :, lanes].astype(F32)
            left_im = cond[1, face, :, lanes].astype(F32)
            left_sum = left_re + left_im
            left_gap = left_im - left_re
            tiles = [None] * (2 * sources)
            for j in range(sources):
                both = jnp.sum((left_re * source32[2, j]).reshape(n_inner // 8, 8, LANES), 0)
                minus = jnp.sum((left_sum * source32[1, j]).reshape(n_inner // 8, 8, LANES), 0)
                plus = jnp.sum((left_gap * source32[0, j]).reshape(n_inner // 8, 8, LANES), 0)
                tiles[j] = both - minus
                tiles[sources + j] = both + plus
            rows[face] = sum_sublanes(tiles)
        parts = [[] for _ in range(owners)]
        at = 0
        while at < n_faces:
            size = owners
            while size > n_faces - at:
                size //= 2
            moved = swap_blocks([rows[at + face] for face in range(size)], CAP)
            for owner in range(owners):
                piece = moved[owner % size]
                skip = owner // size * size * CAP
                if skip:
                    piece = pltpu.roll(piece, LANES - skip, 1)
                parts[owner].append(piece[:, : size * CAP])
            at += size
        for owner in range(owners):
            out[block * owners + owner] = jnp.concatenate(parts[owner], 1).astype(BF16)
    for copy in rest:
        copy.wait()
    position = iota((1, index_rows.shape[1]), 1) % CAP
    for sender in range(index_rows.shape[0]):
        row = index_rows[sender : sender + 1, :]
        index_out[sender : sender + 1, :] = jnp.where(position < counts[sender], row, -1)


def assemble_kernel(received, index_rows, coupling, loads, out):
    peers, rows, face_rows = received.shape
    slots = loads.shape[0] * loads.shape[2]
    width = loads.shape[2]
    slot = iota((slots, face_rows), 0)
    total = jnp.zeros((rows, slots), F32)
    for sender in range(peers):
        onehot = jnp.where(slot == index_rows[sender : sender + 1, :], 1.0, 0.0).astype(BF16)
        total += lax.dot_general(
            received[sender], onehot, (((1,), (1,)), ((), ())), preferred_element_type=F32
        )
    for layer in range(loads.shape[0]):
        loads[layer] = total[:, layer * width : (layer + 1) * width]
    couple_first = coupling[0]
    high = couple_first.astype(BF16).astype(F32)
    extra = jnp.concatenate([high, couple_first - high, jnp.zeros((4, width), F32)], 0)
    block = jnp.concatenate([total[:, :width], extra], 0).astype(BF16)
    for peer in range(out.shape[0]):
        out[peer] = block


def side_by_side(blocks):
    return jnp.concatenate(blocks, 1)


def couple(loads, coupling, carried):
    half = loads.shape[0] // 2
    couple_re, couple_im = coupling[0:1], coupling[1:2]
    real, imag = carried[:half], carried[half:]
    return jnp.concatenate(
        [
            loads[:half] - (couple_re * real - couple_im * imag),
            loads[half:] - (couple_re * imag + couple_im * real),
        ],
        0,
    )


def apply_schur(rhs, schur, layer):
    half = rhs.shape[0] // 2
    first = jnp.dot(rhs, schur[layer, 0], preferred_element_type=F32)
    second = jnp.dot(rhs, schur[layer, 1], preferred_element_type=F32)
    return jnp.concatenate([first[:half] - second[half:], second[:half] + first[half:]], 0)


def round_kernel(*refs, row_at):
    if row_at is None:
        whole, loads, coupling, schur, out, solved_out = refs
    else:
        everyone, whole, loads, coupling, schur, out, solved_out = refs
    peers = whole.shape[0]
    count = loads.shape[1]
    if row_at is not None:
        row = lax.axis_index(row_at)
        start = jnp.maximum(row - 1, 0) * peers
        keep = (row > 0).astype(F32)
    blocks = []
    for peer in range(peers):
        piece = whole[peer].astype(F32)
        pair = piece[count : count + 2] + piece[count + 2 : count + 4]
        if row_at is None:
            before = jnp.zeros((count, piece.shape[1]), F32)
        else:
            before = everyone[start + peer].astype(F32) * keep
        blocks.append(couple(piece[:count], pair, before).astype(BF16))
    solved = apply_schur(jnp.concatenate(blocks, 1), schur, 0)
    solved_out[...] = solved
    block = couple(loads[1], coupling[1], solved).astype(BF16)
    for peer in range(out.shape[0]):
        out[peer] = block


def layer_kernel(gathered, loads, coupling, schur, out, solved_out, *, layer):
    rhs = jnp.concatenate([gathered[peer] for peer in range(gathered.shape[0])], 1)
    solved = apply_schur(rhs, schur, layer)
    solved_out[...] = solved
    block = couple(loads[layer + 1], coupling[layer + 1], solved).astype(BF16)
    for peer in range(out.shape[0]):
        out[peer] = block


def last_kernel(*refs, layer, send):
    gathered, *earlier, schur = refs[: layer + 2]
    outs = refs[layer + 2 :]
    rhs = jnp.concatenate([gathered[peer] for peer in range(gathered.shape[0])], 1)
    solved = apply_schur(rhs, schur, layer)
    for at in range(layer):
        outs[0][at] = earlier[at][...]
    outs[0][layer] = solved
    if send:
        block = solved.astype(BF16)
        for peer in range(outs[1].shape[0]):
            outs[1][peer] = block


def call(kernel, out_shape, operands, scratch=(), space=pltpu.VMEM):
    if space == pltpu.HBM:
        operands = [pltpu.with_memory_space_constraint(operand, space) for operand in operands]
    return pl.pallas_call(
        kernel,
        out_shape=out_shape,
        in_specs=[pl.BlockSpec(memory_space=space)] * len(operands),
        out_specs=jax.tree.map(lambda _: pl.BlockSpec(memory_space=pltpu.VMEM), out_shape),
        scratch_shapes=list(scratch),
        compiler_params=pltpu.CompilerParams(vmem_limit_bytes=16 * 1024 * 1024),
    )(*operands)


def exchange(blocks, axes):
    return lax.all_to_all(blocks, axes, split_axis=0, concat_axis=0, tiled=True)


def shards(cond_block, interior_src, face_index, owner_count, coupling, schur_inv):
    layers = schur_inv.shape[0]
    width = schur_inv.shape[3]
    sources = interior_src.shape[3]
    n_faces, n_inner, elems = cond_block.shape[3:]
    peers = lax.axis_size("xsec")
    chain = lax.axis_size("sweep")
    count = 2 * sources
    struct = jax.ShapeDtypeStruct

    index_rows = face_index[0, 0]
    outgoing, index_rows, coupling, schur_inv = call(
        contract_kernel,
        (
            struct((peers, count, n_faces * CAP), BF16),
            struct(index_rows.shape, index_rows.dtype),
            struct(coupling.shape, coupling.dtype),
            struct(schur_inv.shape, schur_inv.dtype),
        ),
        (cond_block[0, 0], interior_src[0, 0], index_rows, owner_count[0, 0], coupling, schur_inv),
        scratch=(
            pltpu.VMEM(cond_block.shape[2:], BF16),
            pltpu.VMEM(interior_src.shape[2:], BF16),
            pltpu.VMEM(index_rows.shape, index_rows.dtype),
            pltpu.SMEM(owner_count.shape[2:], owner_count.dtype),
            pltpu.VMEM((3, sources, n_inner, LANES), F32),
            pltpu.VMEM((n_faces, count, LANES), F32),
            pltpu.SemaphoreType.DMA((5 + CHUNKS,)),
        ),
        space=pltpu.HBM,
    )
    received = exchange(outgoing, "xsec")
    loads, block = call(
        assemble_kernel,
        (struct((layers, count, width), F32), struct((peers, 16, width), BF16)),
        (received, index_rows, coupling),
    )
    whole = exchange(block, "xsec")
    gathered_shape = struct((peers, count, width), BF16)
    solved_shape = struct((count, width), F32)
    whole_out = struct((layers, count, width), F32)

    def solve_round(everyone, whole, loads, coupling, schur_inv, send):
        behind = () if everyone is None else (everyone,)
        block, solved = call(
            functools.partial(round_kernel, row_at="sweep" if behind else None),
            (gathered_shape, solved_shape),
            behind + (whole, loads, coupling, schur_inv),
        )
        done = [solved]
        for layer in range(1, layers - 1):
            block, solved = call(
                functools.partial(layer_kernel, layer=layer),
                (gathered_shape, solved_shape),
                (exchange(block, "xsec"), loads, coupling, schur_inv),
            )
            done.append(solved)
        sent = (struct((chain * peers, count, width), BF16),) if send else ()
        return call(
            functools.partial(last_kernel, layer=layers - 1, send=send),
            (whole_out,) + sent,
            (exchange(block, "xsec"), *done, schur_inv),
        )

    everyone = solved = None
    for round_at in range(chain - 1):
        solved, block = solve_round(everyone, whole, loads, coupling, schur_inv, True)
        everyone = exchange(block, ("sweep", "xsec"))
    if chain == 1:
        return solve_round(None, whole, loads, coupling, schur_inv, False)[0]
    return lax.cond(
        lax.axis_index("sweep") == chain - 1,
        lambda solved, *rest: solve_round(*rest, False)[0],
        lambda solved, *rest: solved,
        solved, everyone, whole, loads, coupling, schur_inv,
    )


def solution(mesh):
    placed = (
        P("sweep", "xsec", None, None, None, None),
        P("sweep", "xsec", None, None, None, None),
        P("sweep", "xsec", None, None),
        P("sweep", "xsec", None),
        P("sweep", None, "xsec"),
        P("sweep", None, None, "xsec"),
    )
    return jax.shard_map(
        shards, mesh=mesh, in_specs=placed, out_specs=P("sweep", None, "xsec"), check_vma=False
    )
```

```python
import functools

import jax
import jax.numpy as jnp
from jax import lax
from jax.experimental import pallas as pl
from jax.experimental.pallas import tpu as pltpu
from jax.sharding import PartitionSpec as P

CAP = 8
LANES = 128
CHUNKS = 4
F32 = jnp.float32
BF16 = jnp.bfloat16


def iota(shape, axis):
    return lax.broadcasted_iota(jnp.int32, shape, axis)


def sum_sublanes(tiles):
    sub = iota((8, LANES), 0)
    low = sub < 4
    halves = [
        jnp.where(low, tiles[r], tiles[r + 4]) + pltpu.roll(jnp.where(low, tiles[r + 4], tiles[r]), 4, 0)
        for r in range(4)
    ]

    def fold(first, second, step):
        even = (sub & step) == 0
        return jnp.where(even, first, second) + jnp.where(
            even, pltpu.roll(first, 8 - step, 0), pltpu.roll(second, step, 0)
        )

    pairs = [fold(halves[r], halves[r + 2], 2) for r in range(2)]
    return fold(pairs[0], pairs[1], 1)


def swap_blocks(tiles, group):
    lane = iota((8, LANES), 1) // group
    tiles = list(tiles)
    bit = len(tiles) // 2
    while bit:
        here = (lane & bit) == 0
        for at in range(len(tiles)):
            if at & bit == 0:
                low, high = tiles[at], tiles[at + bit]
                tiles[at] = jnp.where(here, low, pltpu.roll(high, bit * group, 1))
                tiles[at + bit] = jnp.where(here, pltpu.roll(low, LANES - bit * group, 1), high)
        bit //= 2
    return tiles


def contract_kernel(
    cond_hbm, source_hbm, index_hbm, counts_hbm, coupling_hbm, schur_hbm,
    out, index_out, coupling_out, schur_out,
    cond, source, index_rows, counts, source32, rows, sems,
):
    _, n_faces, n_inner, elems = cond.shape
    sources = source.shape[1]
    owners = LANES // CAP
    faces_each = n_faces // CHUNKS
    copies = [pltpu.make_async_copy(source_hbm, source, sems.at[0])]
    for chunk in range(CHUNKS):
        some = pl.ds(chunk * faces_each, faces_each)
        copies.append(pltpu.make_async_copy(cond_hbm.at[:, some], cond.at[:, some], sems.at[1 + chunk]))
    rest = [
        pltpu.make_async_copy(index_hbm, index_rows, sems.at[1 + CHUNKS]),
        pltpu.make_async_copy(counts_hbm, counts, sems.at[2 + CHUNKS]),
        pltpu.make_async_copy(coupling_hbm, coupling_out, sems.at[3 + CHUNKS]),
        pltpu.make_async_copy(schur_hbm, schur_out, sems.at[4 + CHUNKS]),
    ]
    for copy in copies + rest:
        copy.start()
    copies[0].wait()
    for block in range(elems // LANES):
        lanes = pl.ds(block * LANES, LANES)
        source32[:2] = source[:, :, :, lanes].astype(F32)
        source32[2] = source32[0] + source32[1]
        for face in range(n_faces):
            if block == 0 and face % faces_each == 0:
                copies[1 + face // faces_each].wait()
            left_re = cond[0, face, :, lanes].astype(F32)
            left_im = cond[1, face, :, lanes].astype(F32)
            left_sum = left_re + left_im
            left_gap = left_im - left_re
            tiles = [None] * (2 * sources)
            for j in range(sources):
                both = jnp.sum((left_re * source32[2, j]).reshape(n_inner // 8, 8, LANES), 0)
                minus = jnp.sum((left_sum * source32[1, j]).reshape(n_inner // 8, 8, LANES), 0)
                plus = jnp.sum((left_gap * source32[0, j]).reshape(n_inner // 8, 8, LANES), 0)
                tiles[j] = both - minus
                tiles[sources + j] = both + plus
            rows[face] = sum_sublanes(tiles)
        parts = [[] for _ in range(owners)]
        at = 0
        while at < n_faces:
            size = owners
            while size > n_faces - at:
                size //= 2
            moved = swap_blocks([rows[at + face] for face in range(size)], CAP)
            for owner in range(owners):
                piece = moved[owner % size]
                skip = owner // size * size * CAP
                if skip:
                    piece = pltpu.roll(piece, LANES - skip, 1)
                parts[owner].append(piece[:, : size * CAP])
            at += size
        for owner in range(owners):
            out[block * owners + owner] = jnp.concatenate(parts[owner], 1).astype(BF16)
    for copy in rest:
        copy.wait()
    position = iota((1, index_rows.shape[1]), 1) % CAP
    for sender in range(index_rows.shape[0]):
        row = index_rows[sender : sender + 1, :]
        index_out[sender : sender + 1, :] = jnp.where(position < counts[sender], row, -1)


def assemble_kernel(received, index_rows, coupling, loads, out):
    peers, rows, face_rows = received.shape
    slots = loads.shape[0] * loads.shape[2]
    width = loads.shape[2]
    slot = iota((slots, face_rows), 0)
    total = jnp.zeros((rows, slots), F32)
    for sender in range(peers):
        onehot = jnp.where(slot == index_rows[sender : sender + 1, :], 1.0, 0.0).astype(BF16)
        total += lax.dot_general(
            received[sender], onehot, (((1,), (1,)), ((), ())), preferred_element_type=F32
        )
    for layer in range(loads.shape[0]):
        loads[layer] = total[:, layer * width : (layer + 1) * width]
    couple_first = coupling[0]
    high = couple_first.astype(BF16).astype(F32)
    extra = jnp.concatenate([high, couple_first - high, jnp.zeros((4, width), F32)], 0)
    block = jnp.concatenate([total[:, :width], extra], 0).astype(BF16)
    for peer in range(out.shape[0]):
        out[peer] = block


def side_by_side(blocks):
    return jnp.concatenate(blocks, 1)


def couple(loads, coupling, carried):
    half = loads.shape[0] // 2
    couple_re, couple_im = coupling[0:1], coupling[1:2]
    real, imag = carried[:half], carried[half:]
    return jnp.concatenate(
        [
            loads[:half] - (couple_re * real - couple_im * imag),
            loads[half:] - (couple_re * imag + couple_im * real),
        ],
        0,
    )


def apply_schur(rhs, schur, layer):
    half = rhs.shape[0] // 2
    first = jnp.dot(rhs, schur[layer, 0], preferred_element_type=F32)
    second = jnp.dot(rhs, schur[layer, 1], preferred_element_type=F32)
    return jnp.concatenate([first[:half] - second[half:], second[:half] + first[half:]], 0)


def round_kernel(*refs, row_at):
    if row_at is None:
        whole, loads, coupling, schur, out, solved_out = refs
    else:
        everyone, whole, loads, coupling, schur, out, solved_out, row_out = refs
    peers = whole.shape[0]
    count = loads.shape[1]
    if row_at is not None:
        row = lax.axis_index(row_at)
        start = jnp.maximum(row - 1, 0) * peers
        keep = (row > 0).astype(F32)
        row_out[0] = row
    blocks = []
    for peer in range(peers):
        piece = whole[peer].astype(F32)
        pair = piece[count : count + 2] + piece[count + 2 : count + 4]
        if row_at is None:
            before = jnp.zeros((count, piece.shape[1]), F32)
        else:
            before = everyone[start + peer].astype(F32) * keep
        blocks.append(couple(piece[:count], pair, before).astype(BF16))
    solved = apply_schur(jnp.concatenate(blocks, 1), schur, 0)
    solved_out[...] = solved
    block = couple(loads[1], coupling[1], solved).astype(BF16)
    for peer in range(out.shape[0]):
        out[peer] = block


def layer_kernel(gathered, loads, coupling, schur, out, solved_out, *, layer):
    rhs = jnp.concatenate([gathered[peer] for peer in range(gathered.shape[0])], 1)
    solved = apply_schur(rhs, schur, layer)
    solved_out[...] = solved
    block = couple(loads[layer + 1], coupling[layer + 1], solved).astype(BF16)
    for peer in range(out.shape[0]):
        out[peer] = block


def last_kernel(*refs, layer, send):
    gathered, *earlier, schur = refs[: layer + 2]
    outs = refs[layer + 2 :]
    rhs = jnp.concatenate([gathered[peer] for peer in range(gathered.shape[0])], 1)
    solved = apply_schur(rhs, schur, layer)
    for at in range(layer):
        outs[0][at] = earlier[at][...]
    outs[0][layer] = solved
    if send:
        block = solved.astype(BF16)
        for peer in range(outs[1].shape[0]):
            outs[1][peer] = block


def call(kernel, out_shape, operands, scratch=(), space=pltpu.VMEM):
    if space == pltpu.HBM:
        operands = [pltpu.with_memory_space_constraint(operand, space) for operand in operands]
    return pl.pallas_call(
        kernel,
        out_shape=out_shape,
        in_specs=[pl.BlockSpec(memory_space=space)] * len(operands),
        out_specs=jax.tree.map(
            lambda out: pl.BlockSpec(memory_space=getattr(out, "memory_space", None) or pltpu.VMEM), out_shape
        ),
        scratch_shapes=list(scratch),
        compiler_params=pltpu.CompilerParams(vmem_limit_bytes=16 * 1024 * 1024),
    )(*operands)


def exchange(blocks, axes):
    return lax.all_to_all(blocks, axes, split_axis=0, concat_axis=0, tiled=True)


def shards(cond_block, interior_src, face_index, owner_count, coupling, schur_inv):
    layers = schur_inv.shape[0]
    width = schur_inv.shape[3]
    sources = interior_src.shape[3]
    n_faces, n_inner, elems = cond_block.shape[3:]
    peers = lax.axis_size("xsec")
    chain = lax.axis_size("sweep")
    count = 2 * sources
    struct = jax.ShapeDtypeStruct

    index_rows = face_index[0, 0]
    outgoing, index_rows, coupling, schur_inv = call(
        contract_kernel,
        (
            struct((peers, count, n_faces * CAP), BF16),
            struct(index_rows.shape, index_rows.dtype),
            struct(coupling.shape, coupling.dtype),
            struct(schur_inv.shape, schur_inv.dtype),
        ),
        (cond_block[0, 0], interior_src[0, 0], index_rows, owner_count[0, 0], coupling, schur_inv),
        scratch=(
            pltpu.VMEM(cond_block.shape[2:], BF16),
            pltpu.VMEM(interior_src.shape[2:], BF16),
            pltpu.VMEM(index_rows.shape, index_rows.dtype),
            pltpu.SMEM(owner_count.shape[2:], owner_count.dtype),
            pltpu.VMEM((3, sources, n_inner, LANES), F32),
            pltpu.VMEM((n_faces, count, LANES), F32),
            pltpu.SemaphoreType.DMA((5 + CHUNKS,)),
        ),
        space=pltpu.HBM,
    )
    received = exchange(outgoing, "xsec")
    loads, block = call(
        assemble_kernel,
        (struct((layers, count, width), F32), struct((peers, 16, width), BF16)),
        (received, index_rows, coupling),
    )
    whole = exchange(block, "xsec")
    gathered_shape = struct((peers, count, width), BF16)
    solved_shape = struct((count, width), F32)
    whole_out = pltpu.VMEM((layers, count, width), F32)

    def first_layer(everyone, *operands):
        if everyone is None:
            return call(
                functools.partial(round_kernel, row_at=None), (gathered_shape, solved_shape), operands
            )
        return call(
            functools.partial(round_kernel, row_at="sweep"),
            (gathered_shape, solved_shape, pltpu.SMEM((1,), jnp.int32)),
            (everyone, *operands),
        )

    def other_layers(block, solved, loads, coupling, schur_inv, send):
        done = [solved]
        for layer in range(1, layers - 1):
            block, solved = call(
                functools.partial(layer_kernel, layer=layer),
                (gathered_shape, solved_shape),
                (exchange(block, "xsec"), loads, coupling, schur_inv),
            )
            done.append(solved)
        sent = (struct((chain * peers, count, width), BF16),) if send else ()
        return call(
            functools.partial(last_kernel, layer=layers - 1, send=send),
            (whole_out,) + sent,
            (exchange(block, "xsec"), *done, schur_inv),
        )

    everyone = None
    for round_at in range(chain - 1):
        block, solved = first_layer(everyone, whole, loads, coupling, schur_inv)[:2]
        finished, block = other_layers(block, solved, loads, coupling, schur_inv, True)
        everyone = exchange(block, ("sweep", "xsec"))
    if chain == 1:
        block, solved = first_layer(None, whole, loads, coupling, schur_inv)
        return other_layers(block, solved, loads, coupling, schur_inv, False)[0]
    block, solved, row = first_layer(everyone, whole, loads, coupling, schur_inv)
    return lax.cond(
        row[0] == chain - 1,
        lambda finished, *rest: other_layers(*rest, False)[0],
        lambda finished, *rest: finished,
        finished, block, solved, loads, coupling, schur_inv,
    )


def solution(mesh):
    placed = (
        P("sweep", "xsec", None, None, None, None),
        P("sweep", "xsec", None, None, None, None),
        P("sweep", "xsec", None, None),
        P("sweep", "xsec", None),
        P("sweep", None, "xsec"),
        P("sweep", None, None, "xsec"),
    )
    return jax.shard_map(
        shards, mesh=mesh, in_specs=placed, out_specs=P("sweep", None, "xsec"), check_vma=False
    )
```

```python
import functools

import jax
import jax.numpy as jnp
from jax import lax
from jax.experimental import pallas as pl
from jax.experimental.pallas import tpu as pltpu
from jax.sharding import PartitionSpec as P

CAP = 8
LANES = 128
CHUNKS = 2
F32 = jnp.float32
BF16 = jnp.bfloat16


def iota(shape, axis):
    return lax.broadcasted_iota(jnp.int32, shape, axis)


def sum_sublanes(tiles):
    sub = iota((8, LANES), 0)
    low = sub < 4
    halves = [
        jnp.where(low, tiles[r], tiles[r + 4]) + pltpu.roll(jnp.where(low, tiles[r + 4], tiles[r]), 4, 0)
        for r in range(4)
    ]

    def fold(first, second, step):
        even = (sub & step) == 0
        return jnp.where(even, first, second) + jnp.where(
            even, pltpu.roll(first, 8 - step, 0), pltpu.roll(second, step, 0)
        )

    pairs = [fold(halves[r], halves[r + 2], 2) for r in range(2)]
    return fold(pairs[0], pairs[1], 1)


def skew_block(tile, at, group):
    shift = at * group % LANES
    return pltpu.roll(tile, shift, 1) if shift else tile


def unskew_blocks(tiles, group):
    count = len(tiles)
    lane = iota((8, LANES), 1) // group
    tiles = list(tiles)
    bit = 1
    while bit < count:
        take = (lane & bit) != 0
        tiles = [jnp.where(take, tiles[(at + bit) % count], tiles[at]) for at in range(count)]
        bit *= 2
    return [skew_block(tiles[-at % count], LANES // group - at, group) for at in range(count)]


def pack_coupling(layer, rows):
    high = layer.astype(BF16).astype(F32)
    both = jnp.concatenate([high, layer - high], 0)
    lanes = both.shape[0] * both.shape[1] // rows
    return jnp.concatenate([both[:, at : at + lanes] for at in range(0, both.shape[1], lanes)], 0)


def unpack_coupling(packed):
    both = jnp.concatenate([packed[at : at + 4] for at in range(0, packed.shape[0], 4)], 1)
    return both[:2] + both[2:]


def contract_kernel(
    cond_hbm, source_hbm, index_hbm, counts_hbm, coupling_hbm, schur_hbm,
    out, place_out, layer_out, coupling_out, schur_out,
    cond, source, index_rows, counts, source32, sems,
):
    _, n_faces, n_inner, elems = cond.shape
    sources = source.shape[1]
    owners = LANES // CAP
    faces_each = n_faces // CHUNKS
    width = coupling_out.shape[2]
    groups = []
    while len(groups) < n_faces:
        size = owners
        while size > n_faces - len(groups):
            size //= 2
        groups += [(len(groups), size)] * size
    early = [
        pltpu.make_async_copy(source_hbm, source, sems.at[0]),
        pltpu.make_async_copy(index_hbm, index_rows, sems.at[1]),
        pltpu.make_async_copy(counts_hbm, counts, sems.at[2]),
    ]
    chunks = []
    for chunk in range(CHUNKS):
        some = pl.ds(chunk * faces_each, faces_each)
        chunks.append(pltpu.make_async_copy(cond_hbm.at[:, some], cond.at[:, some], sems.at[3 + chunk]))
    late = [
        pltpu.make_async_copy(coupling_hbm, coupling_out, sems.at[3 + CHUNKS]),
        pltpu.make_async_copy(schur_hbm, schur_out, sems.at[4 + CHUNKS]),
    ]
    for copy in early + chunks + late:
        copy.start()
    for copy in early:
        copy.wait()
    position = iota((1, index_rows.shape[1]), 1) % CAP
    for sender in range(index_rows.shape[0]):
        row = index_rows[sender : sender + 1, :]
        live = position < counts[sender]
        place_out[sender : sender + 1, :] = jnp.where(live, row % width, -1)
        layer_out[sender : sender + 1, :] = row // width
    for block in range(elems // LANES):
        lanes = pl.ds(block * LANES, LANES)
        source32[:2] = source[:, :, :, lanes].astype(F32)
        source32[2] = source32[0] + source32[1]
        parts = [[] for _ in range(owners)]
        skewed = []
        for face in range(n_faces):
            if block == 0 and face % faces_each == 0:
                chunks[face // faces_each].wait()
            left_re = cond[0, face, :, lanes].astype(F32)
            left_im = cond[1, face, :, lanes].astype(F32)
            left_sum = left_re + left_im
            left_gap = left_im - left_re
            tiles = [None] * (2 * sources)
            for j in range(sources):
                both = jnp.sum((left_re * source32[2, j]).reshape(n_inner // 8, 8, LANES), 0)
                minus = jnp.sum((left_sum * source32[1, j]).reshape(n_inner // 8, 8, LANES), 0)
                plus = jnp.sum((left_gap * source32[0, j]).reshape(n_inner // 8, 8, LANES), 0)
                tiles[j] = both - minus
                tiles[sources + j] = both + plus
            first, size = groups[face]
            skewed.append(skew_block(sum_sublanes(tiles), face - first, CAP))
            if len(skewed) < size:
                continue
            moved = unskew_blocks(skewed, CAP)
            skewed = []
            for owner in range(owners):
                piece = moved[owner % size]
                if owner >= size:
                    piece = skew_block(piece, owners - owner // size * size, CAP)
                parts[owner].append(piece[:, : size * CAP])
        if block == 0:
            late[0].wait()
            spare = pack_coupling(coupling_out[0], 2 * sources)
        for owner in range(owners):
            out[block * owners + owner] = jnp.concatenate(parts[owner] + [spare], 1).astype(BF16)
    late[1].wait()


def assemble_kernel(received, place_rows, layer_rows, coupling, loads, out):
    peers, rows, _ = received.shape
    face_rows = place_rows.shape[1]
    layers, _, width = loads.shape
    place = iota((width, face_rows), 0)
    total = jnp.zeros((layers * rows, width), F32)
    for sender in range(peers):
        onehot = jnp.where(place == place_rows[sender : sender + 1, :], 1.0, 0.0).astype(BF16)
        values = received[sender].astype(F32)[:, :face_rows]
        layer_row = layer_rows[sender : sender + 1, :]
        split = [jnp.where(layer_row == layer, values, 0.0) for layer in range(layers)]
        total += lax.dot_general(
            jnp.concatenate(split, 0).astype(BF16), onehot, (((1,), (1,)), ((), ())), preferred_element_type=F32
        )
    for layer in range(layers):
        loads[layer] = total[layer * rows : (layer + 1) * rows]
    block = couple(total[:rows], coupling[0], jnp.zeros((rows, width), F32)).astype(BF16)
    for peer in range(out.shape[0]):
        out[peer] = block


def couple(loads, coupling, carried):
    half = loads.shape[0] // 2
    couple_re, couple_im = coupling[0:1], coupling[1:2]
    real, imag = carried[:half], carried[half:]
    return jnp.concatenate(
        [
            loads[:half] - (couple_re * real - couple_im * imag),
            loads[half:] - (couple_re * imag + couple_im * real),
        ],
        0,
    )


def apply_schur(rhs, schur, layer):
    half = rhs.shape[0] // 2
    first = jnp.dot(rhs, schur[layer, 0], preferred_element_type=F32)
    second = jnp.dot(rhs, schur[layer, 1], preferred_element_type=F32)
    return jnp.concatenate([first[:half] - second[half:], second[:half] + first[half:]], 0)


def cross_kernel(everyone, whole, received, loads, coupling, schur, out, solved_out, row_out, *, row_axis):
    peers = whole.shape[0]
    _, count, width = loads.shape
    spare = received.shape[2] - 4 * width // count
    row = lax.axis_index(row_axis)
    row_out[0] = row
    start = jnp.maximum(row - 1, 0) * peers
    keep = (row > 0).astype(F32)
    blocks = []
    for peer in range(peers):
        pair = unpack_coupling(received[peer].astype(F32)[:, spare:])
        before = everyone[start + peer].astype(F32) * keep
        blocks.append(couple(whole[peer].astype(F32), pair, before).astype(BF16))
    solved = apply_schur(jnp.concatenate(blocks, 1), schur, 0)
    solved_out[...] = solved
    block = couple(loads[1], coupling[1], solved).astype(BF16)
    for peer in range(out.shape[0]):
        out[peer] = block


def layer_kernel(gathered, loads, coupling, schur, out, solved_out, *, layer):
    rhs = jnp.concatenate([gathered[peer] for peer in range(gathered.shape[0])], 1)
    solved = apply_schur(rhs, schur, layer)
    solved_out[...] = solved
    block = couple(loads[layer + 1], coupling[layer + 1], solved).astype(BF16)
    for peer in range(out.shape[0]):
        out[peer] = block


def last_kernel(*refs, layer, send):
    gathered, *earlier, schur = refs[: layer + 2]
    outs = refs[layer + 2 :]
    rhs = jnp.concatenate([gathered[peer] for peer in range(gathered.shape[0])], 1)
    solved = apply_schur(rhs, schur, layer)
    for at in range(layer):
        outs[0][at] = earlier[at][...]
    outs[0][layer] = solved
    if send:
        block = solved.astype(BF16)
        for peer in range(outs[1].shape[0]):
            outs[1][peer] = block


def call(kernel, out_shape, operands, scratch=(), space=pltpu.VMEM):
    if space == pltpu.HBM:
        operands = [pltpu.with_memory_space_constraint(operand, space) for operand in operands]
    return pl.pallas_call(
        kernel,
        out_shape=out_shape,
        in_specs=[pl.BlockSpec(memory_space=space)] * len(operands),
        out_specs=jax.tree.map(
            lambda out: pl.BlockSpec(memory_space=getattr(out, "memory_space", None) or pltpu.VMEM), out_shape
        ),
        scratch_shapes=list(scratch),
        compiler_params=pltpu.CompilerParams(vmem_limit_bytes=16 * 1024 * 1024),
    )(*operands)


def exchange(blocks, axes):
    return lax.all_to_all(blocks, axes, split_axis=0, concat_axis=0, tiled=True)


def shards(cond_block, interior_src, face_index, owner_count, coupling, schur_inv):
    layers = schur_inv.shape[0]
    width = schur_inv.shape[3]
    sources = interior_src.shape[3]
    n_faces, n_inner, elems = cond_block.shape[3:]
    peers = lax.axis_size("xsec")
    chain = lax.axis_size("sweep")
    count = 2 * sources
    struct = jax.ShapeDtypeStruct
    gathered_shape = struct((peers, count, width), BF16)

    index_rows = face_index[0, 0]
    outgoing, place_rows, layer_rows, coupling, schur_inv = call(
        contract_kernel,
        (
            struct((peers, count, n_faces * CAP + 4 * width // count), BF16),
            struct(index_rows.shape, index_rows.dtype),
            struct(index_rows.shape, index_rows.dtype),
            struct(coupling.shape, coupling.dtype),
            struct(schur_inv.shape, schur_inv.dtype),
        ),
        (cond_block[0, 0], interior_src[0, 0], index_rows, owner_count[0, 0], coupling, schur_inv),
        scratch=(
            pltpu.VMEM(cond_block.shape[2:], BF16),
            pltpu.VMEM(interior_src.shape[2:], BF16),
            pltpu.VMEM(index_rows.shape, index_rows.dtype),
            pltpu.SMEM(owner_count.shape[2:], owner_count.dtype),
            pltpu.VMEM((3, sources, n_inner, LANES), F32),
            pltpu.SemaphoreType.DMA((5 + CHUNKS,)),
        ),
        space=pltpu.HBM,
    )
    received = exchange(outgoing, "xsec")
    loads, block = call(
        assemble_kernel,
        (struct((layers, count, width), F32), gathered_shape),
        (received, place_rows, layer_rows, coupling),
    )
    whole = exchange(block, "xsec")
    solved_shape = struct((count, width), F32)
    whole_out = pltpu.VMEM((layers, count, width), F32)

    def next_layers(gathered, loads, coupling, schur_inv, done, send):
        for layer in range(len(done), layers - 1):
            block, solved = call(
                functools.partial(layer_kernel, layer=layer),
                (gathered_shape, solved_shape),
                (gathered, loads, coupling, schur_inv),
            )
            done = done + [solved]
            gathered = exchange(block, "xsec")
        sent = (struct((chain * peers, count, width), BF16),) if send else ()
        return call(
            functools.partial(last_kernel, layer=layers - 1, send=send),
            (whole_out,) + sent,
            (gathered, *done, schur_inv),
        )

    def later_round(everyone):
        return call(
            functools.partial(cross_kernel, row_axis="sweep"),
            (gathered_shape, solved_shape, pltpu.SMEM((1,), jnp.int32)),
            (everyone, whole, received, loads, coupling, schur_inv),
        )

    if chain == 1:
        return next_layers(whole, loads, coupling, schur_inv, [], False)[0]
    finished, block = next_layers(whole, loads, coupling, schur_inv, [], True)
    for _ in range(chain - 2):
        block, solved, _ = later_round(exchange(block, ("sweep", "xsec")))
        finished, block = next_layers(
            exchange(block, "xsec"), loads, coupling, schur_inv, [solved], True
        )
    block, solved, row = later_round(exchange(block, ("sweep", "xsec")))

    def last_round(finished, block, solved, loads, coupling, schur_inv):
        return next_layers(exchange(block, "xsec"), loads, coupling, schur_inv, [solved], False)[0]

    return lax.cond(
        row[0] == chain - 1,
        last_round,
        lambda finished, *rest: finished,
        finished, block, solved, loads, coupling, schur_inv,
    )


def solution(mesh):
    placed = (
        P("sweep", "xsec", None, None, None, None),
        P("sweep", "xsec", None, None, None, None),
        P("sweep", "xsec", None, None),
        P("sweep", "xsec", None),
        P("sweep", None, "xsec"),
        P("sweep", None, None, "xsec"),
    )
    return jax.shard_map(
        shards, mesh=mesh, in_specs=placed, out_specs=P("sweep", None, "xsec"), check_vma=False
    )
```

```python
import functools

import jax
import jax.numpy as jnp
from jax import lax
from jax.experimental import pallas as pl
from jax.experimental.pallas import tpu as pltpu
from jax.sharding import PartitionSpec as P

CAP = 8
LANES = 128
CHUNKS = 2
F32 = jnp.float32
BF16 = jnp.bfloat16


def first_of(count):
    return (count // 2 + 1) % count


def place_of(device, count):
    return (device - first_of(count)) % count


def iota(shape, axis):
    return lax.broadcasted_iota(jnp.int32, shape, axis)


def sum_sublanes(tiles):
    sub = iota((8, LANES), 0)
    low = sub < 4
    halves = [
        jnp.where(low, tiles[r], tiles[r + 4]) + pltpu.roll(jnp.where(low, tiles[r + 4], tiles[r]), 4, 0)
        for r in range(4)
    ]

    def fold(first, second, step):
        even = (sub & step) == 0
        return jnp.where(even, first, second) + jnp.where(
            even, pltpu.roll(first, 8 - step, 0), pltpu.roll(second, step, 0)
        )

    pairs = [fold(halves[r], halves[r + 2], 2) for r in range(2)]
    return fold(pairs[0], pairs[1], 1)


def skew_block(tile, at, group):
    shift = at * group % LANES
    return pltpu.roll(tile, shift, 1) if shift else tile


def unskew_blocks(tiles, group):
    count = len(tiles)
    lane = iota((8, LANES), 1) // group
    tiles = list(tiles)
    bit = 1
    while bit < count:
        take = (lane & bit) != 0
        tiles = [jnp.where(take, tiles[(at + bit) % count], tiles[at]) for at in range(count)]
        bit *= 2
    return [skew_block(tiles[-at % count], LANES // group - at, group) for at in range(count)]


def pack_coupling(layer, rows):
    high = layer.astype(BF16).astype(F32)
    both = jnp.concatenate([high, layer - high], 0)
    lanes = both.shape[0] * both.shape[1] // rows
    return jnp.concatenate([both[:, at : at + lanes] for at in range(0, both.shape[1], lanes)], 0)


def unpack_coupling(packed):
    both = jnp.concatenate([packed[at : at + 4] for at in range(0, packed.shape[0], 4)], 1)
    return both[:2] + both[2:]


def contract_kernel(
    cond_hbm, source_hbm, index_hbm, counts_hbm, coupling_hbm, schur_hbm,
    out, place_out, layer_out, coupling_out, schur_out,
    cond, source, index_rows, counts, source32, sems,
):
    _, n_faces, n_inner, elems = cond.shape
    sources = source.shape[1]
    owners = LANES // CAP
    faces_each = n_faces // CHUNKS
    width = coupling_out.shape[2]
    groups = []
    while len(groups) < n_faces:
        size = owners
        while size > n_faces - len(groups):
            size //= 2
        groups += [(len(groups), size)] * size
    early = [
        pltpu.make_async_copy(source_hbm, source, sems.at[0]),
        pltpu.make_async_copy(index_hbm, index_rows, sems.at[1]),
        pltpu.make_async_copy(counts_hbm, counts, sems.at[2]),
    ]
    chunks = []
    for chunk in range(CHUNKS):
        some = pl.ds(chunk * faces_each, faces_each)
        chunks.append(pltpu.make_async_copy(cond_hbm.at[:, some], cond.at[:, some], sems.at[3 + chunk]))
    late = [
        pltpu.make_async_copy(coupling_hbm, coupling_out, sems.at[3 + CHUNKS]),
        pltpu.make_async_copy(schur_hbm, schur_out, sems.at[4 + CHUNKS]),
    ]
    for copy in early + chunks + late:
        copy.start()
    for copy in early:
        copy.wait()
    position = iota((1, index_rows.shape[1]), 1) % CAP
    for sender in range(index_rows.shape[0]):
        row = index_rows[sender : sender + 1, :]
        live = position < counts[sender]
        place_out[sender : sender + 1, :] = jnp.where(live, row % width, -1)
        layer_out[sender : sender + 1, :] = row // width
    for block in range(elems // LANES):
        lanes = pl.ds(block * LANES, LANES)
        source32[:2] = source[:, :, :, lanes].astype(F32)
        source32[2] = source32[0] + source32[1]
        parts = [[] for _ in range(owners)]
        skewed = []
        for face in range(n_faces):
            if block == 0 and face % faces_each == 0:
                chunks[face // faces_each].wait()
            left_re = cond[0, face, :, lanes].astype(F32)
            left_im = cond[1, face, :, lanes].astype(F32)
            left_sum = left_re + left_im
            left_gap = left_im - left_re
            tiles = [None] * (2 * sources)
            for j in range(sources):
                both = jnp.sum((left_re * source32[2, j]).reshape(n_inner // 8, 8, LANES), 0)
                minus = jnp.sum((left_sum * source32[1, j]).reshape(n_inner // 8, 8, LANES), 0)
                plus = jnp.sum((left_gap * source32[0, j]).reshape(n_inner // 8, 8, LANES), 0)
                tiles[j] = both - minus
                tiles[sources + j] = both + plus
            first, size = groups[face]
            skewed.append(skew_block(sum_sublanes(tiles), face - first, CAP))
            if len(skewed) < size:
                continue
            moved = unskew_blocks(skewed, CAP)
            skewed = []
            for owner in range(owners):
                piece = moved[owner % size]
                if owner >= size:
                    piece = skew_block(piece, owners - owner // size * size, CAP)
                parts[owner].append(piece[:, : size * CAP])
        if block == 0:
            late[0].wait()
            spare = pack_coupling(coupling_out[0], 2 * sources)
        for owner in range(owners):
            out[place_of(block * owners + owner, out.shape[0])] = jnp.concatenate(parts[owner] + [spare], 1).astype(BF16)
    late[1].wait()


def assemble_kernel(received, place_rows, layer_rows, coupling, loads, out):
    peers, rows, _ = received.shape
    face_rows = place_rows.shape[1]
    layers, _, width = loads.shape
    place = iota((width, face_rows), 0)
    total = jnp.zeros((layers * rows, width), F32)
    for sender in range(peers):
        onehot = jnp.where(place == place_rows[sender : sender + 1, :], 1.0, 0.0).astype(BF16)
        values = received[place_of(sender, peers)].astype(F32)[:, :face_rows]
        layer_row = layer_rows[sender : sender + 1, :]
        split = [jnp.where(layer_row == layer, values, 0.0) for layer in range(layers)]
        total += lax.dot_general(
            jnp.concatenate(split, 0).astype(BF16), onehot, (((1,), (1,)), ((), ())), preferred_element_type=F32
        )
    for layer in range(layers):
        loads[layer] = total[layer * rows : (layer + 1) * rows]
    block = couple(total[:rows], coupling[0], jnp.zeros((rows, width), F32)).astype(BF16)
    for peer in range(out.shape[0]):
        out[peer] = block


def couple(loads, coupling, carried):
    half = loads.shape[0] // 2
    couple_re, couple_im = coupling[0:1], coupling[1:2]
    real, imag = carried[:half], carried[half:]
    return jnp.concatenate(
        [
            loads[:half] - (couple_re * real - couple_im * imag),
            loads[half:] - (couple_re * imag + couple_im * real),
        ],
        0,
    )


def apply_schur(rhs, schur, layer):
    half = rhs.shape[0] // 2
    first = jnp.dot(rhs, schur[layer, 0], preferred_element_type=F32)
    second = jnp.dot(rhs, schur[layer, 1], preferred_element_type=F32)
    return jnp.concatenate([first[:half] - second[half:], second[:half] + first[half:]], 0)


def cross_kernel(everyone, whole, received, loads, coupling, schur, out, solved_out, row_out, *, row_axis):
    peers = whole.shape[0]
    _, count, width = loads.shape
    spare = received.shape[2] - 4 * width // count
    row = lax.axis_index(row_axis)
    row_out[0] = row
    start = jnp.maximum(row - 1, 0) * peers
    keep = (row > 0).astype(F32)
    blocks = []
    for peer in range(peers):
        place = place_of(peer, peers)
        pair = unpack_coupling(received[place].astype(F32)[:, spare:])
        before = everyone[start + peer].astype(F32) * keep
        blocks.append(couple(whole[place].astype(F32), pair, before).astype(BF16))
    solved = apply_schur(jnp.concatenate(blocks, 1), schur, 0)
    solved_out[...] = solved
    block = couple(loads[1], coupling[1], solved).astype(BF16)
    for peer in range(out.shape[0]):
        out[peer] = block


def side_by_side(gathered):
    count = gathered.shape[0]
    return jnp.concatenate([gathered[place_of(peer, count)] for peer in range(count)], 1)


def layer_kernel(gathered, loads, coupling, schur, out, solved_out, *, layer):
    rhs = side_by_side(gathered)
    solved = apply_schur(rhs, schur, layer)
    solved_out[...] = solved
    block = couple(loads[layer + 1], coupling[layer + 1], solved).astype(BF16)
    for peer in range(out.shape[0]):
        out[peer] = block


def last_kernel(*refs, layer, send):
    gathered, *earlier, schur = refs[: layer + 2]
    outs = refs[layer + 2 :]
    rhs = side_by_side(gathered)
    solved = apply_schur(rhs, schur, layer)
    for at in range(layer):
        outs[0][at] = earlier[at][...]
    outs[0][layer] = solved
    if send:
        block = solved.astype(BF16)
        for peer in range(outs[1].shape[0]):
            outs[1][peer] = block


def call(kernel, out_shape, operands, scratch=(), space=pltpu.VMEM):
    if space == pltpu.HBM:
        operands = [pltpu.with_memory_space_constraint(operand, space) for operand in operands]
    return pl.pallas_call(
        kernel,
        out_shape=out_shape,
        in_specs=[pl.BlockSpec(memory_space=space)] * len(operands),
        out_specs=jax.tree.map(
            lambda out: pl.BlockSpec(memory_space=getattr(out, "memory_space", None) or pltpu.VMEM), out_shape
        ),
        scratch_shapes=list(scratch),
        compiler_params=pltpu.CompilerParams(vmem_limit_bytes=16 * 1024 * 1024),
    )(*operands)


def exchange_row(blocks):
    count = blocks.shape[0]
    order = [(first_of(count) + place) % count for place in range(count)]
    return lax.all_to_all(
        blocks, "xsec", split_axis=0, concat_axis=0, tiled=True, axis_index_groups=[order]
    )


def exchange_all(blocks):
    return lax.all_to_all(blocks, ("sweep", "xsec"), split_axis=0, concat_axis=0, tiled=True)


def shards(cond_block, interior_src, face_index, owner_count, coupling, schur_inv):
    layers = schur_inv.shape[0]
    width = schur_inv.shape[3]
    sources = interior_src.shape[3]
    n_faces, n_inner, elems = cond_block.shape[3:]
    peers = lax.axis_size("xsec")
    chain = lax.axis_size("sweep")
    count = 2 * sources
    struct = jax.ShapeDtypeStruct
    gathered_shape = struct((peers, count, width), BF16)

    index_rows = face_index[0, 0]
    outgoing, place_rows, layer_rows, coupling, schur_inv = call(
        contract_kernel,
        (
            struct((peers, count, n_faces * CAP + 4 * width // count), BF16),
            struct(index_rows.shape, index_rows.dtype),
            struct(index_rows.shape, index_rows.dtype),
            struct(coupling.shape, coupling.dtype),
            struct(schur_inv.shape, schur_inv.dtype),
        ),
        (cond_block[0, 0], interior_src[0, 0], index_rows, owner_count[0, 0], coupling, schur_inv),
        scratch=(
            pltpu.VMEM(cond_block.shape[2:], BF16),
            pltpu.VMEM(interior_src.shape[2:], BF16),
            pltpu.VMEM(index_rows.shape, index_rows.dtype),
            pltpu.SMEM(owner_count.shape[2:], owner_count.dtype),
            pltpu.VMEM((3, sources, n_inner, LANES), F32),
            pltpu.SemaphoreType.DMA((5 + CHUNKS,)),
        ),
        space=pltpu.HBM,
    )
    received = exchange_row(outgoing)
    loads, block = call(
        assemble_kernel,
        (struct((layers, count, width), F32), gathered_shape),
        (received, place_rows, layer_rows, coupling),
    )
    whole = exchange_row(block)
    solved_shape = struct((count, width), F32)
    whole_out = pltpu.VMEM((layers, count, width), F32)

    def next_layers(gathered, loads, coupling, schur_inv, done, send):
        for layer in range(len(done), layers - 1):
            block, solved = call(
                functools.partial(layer_kernel, layer=layer),
                (gathered_shape, solved_shape),
                (gathered, loads, coupling, schur_inv),
            )
            done = done + [solved]
            gathered = exchange_row(block)
        sent = (struct((chain * peers, count, width), BF16),) if send else ()
        return call(
            functools.partial(last_kernel, layer=layers - 1, send=send),
            (whole_out,) + sent,
            (gathered, *done, schur_inv),
        )

    def later_round(everyone):
        return call(
            functools.partial(cross_kernel, row_axis="sweep"),
            (gathered_shape, solved_shape, pltpu.SMEM((1,), jnp.int32)),
            (everyone, whole, received, loads, coupling, schur_inv),
        )

    if chain == 1:
        return next_layers(whole, loads, coupling, schur_inv, [], False)[0]
    finished, block = next_layers(whole, loads, coupling, schur_inv, [], True)
    for _ in range(chain - 2):
        block, solved, _ = later_round(exchange_all(block))
        finished, block = next_layers(
            exchange_row(block), loads, coupling, schur_inv, [solved], True
        )
    block, solved, row = later_round(exchange_all(block))

    def last_round(finished, block, solved, loads, coupling, schur_inv):
        return next_layers(exchange_row(block), loads, coupling, schur_inv, [solved], False)[0]

    return lax.cond(
        row[0] == chain - 1,
        last_round,
        lambda finished, *rest: finished,
        finished, block, solved, loads, coupling, schur_inv,
    )


def solution(mesh):
    placed = (
        P("sweep", "xsec", None, None, None, None),
        P("sweep", "xsec", None, None, None, None),
        P("sweep", "xsec", None, None),
        P("sweep", "xsec", None),
        P("sweep", None, "xsec"),
        P("sweep", None, None, "xsec"),
    )
    return jax.shard_map(
        shards, mesh=mesh, in_specs=placed, out_specs=P("sweep", None, "xsec"), check_vma=False
    )
```

```python
import functools

import jax
import jax.numpy as jnp
from jax import lax
from jax.experimental import pallas as pl
from jax.experimental.pallas import tpu as pltpu
from jax.sharding import PartitionSpec as P

CAP = 8
LANES = 128
CHUNKS = 2
F32 = jnp.float32
BF16 = jnp.bfloat16


def first_of(count):
    return (count // 2 + 1) % count


def place_of(device, count):
    return (device - first_of(count)) % count


def iota(shape, axis):
    return lax.broadcasted_iota(jnp.int32, shape, axis)


def sum_sublanes(tiles):
    sub = iota((8, LANES), 0)
    low = sub < 4
    halves = [
        jnp.where(low, tiles[r], tiles[r + 4]) + pltpu.roll(jnp.where(low, tiles[r + 4], tiles[r]), 4, 0)
        for r in range(4)
    ]

    def fold(first, second, step):
        even = (sub & step) == 0
        return jnp.where(even, first, second) + jnp.where(
            even, pltpu.roll(first, 8 - step, 0), pltpu.roll(second, step, 0)
        )

    pairs = [fold(halves[r], halves[r + 2], 2) for r in range(2)]
    return fold(pairs[0], pairs[1], 1)


def skew_block(tile, at, group):
    shift = at * group % LANES
    return pltpu.roll(tile, shift, 1) if shift else tile


def unskew_blocks(tiles, group):
    count = len(tiles)
    lane = iota((8, LANES), 1)
    tiles = list(tiles)
    bit = 1
    while bit < count:
        take = (lane & (bit * group)) != 0
        tiles = [jnp.where(take, tiles[(at + bit) % count], tiles[at]) for at in range(count)]
        bit *= 2
    return [skew_block(tiles[-at % count], LANES // group - at, group) for at in range(count)]


def pack_coupling(layer, rows):
    high = layer.astype(BF16).astype(F32)
    both = jnp.concatenate([high, layer - high], 0)
    lanes = both.shape[0] * both.shape[1] // rows
    return jnp.concatenate([both[:, at : at + lanes] for at in range(0, both.shape[1], lanes)], 0)


def unpack_coupling(packed):
    both = jnp.concatenate([packed[at : at + 4] for at in range(0, packed.shape[0], 4)], 1)
    return both[:2] + both[2:]


def contract_kernel(
    cond_hbm, source_hbm, index_hbm, counts_hbm, coupling_hbm, schur_hbm,
    out, place_out, layer_out, coupling_out, schur_out,
    cond, source, index_rows, counts, source32, sems,
):
    _, n_faces, n_inner, elems = cond.shape
    sources = source.shape[1]
    owners = LANES // CAP
    faces_each = n_faces // CHUNKS
    layers, _, width = coupling_out.shape
    groups = []
    while len(groups) < n_faces:
        size = owners
        while size > n_faces - len(groups):
            size //= 2
        groups += [(len(groups), size)] * size
    early = [
        pltpu.make_async_copy(source_hbm, source, sems.at[0]),
        pltpu.make_async_copy(index_hbm, index_rows, sems.at[1]),
        pltpu.make_async_copy(counts_hbm, counts, sems.at[2]),
    ]
    chunks = []
    for chunk in range(CHUNKS):
        some = pl.ds(chunk * faces_each, faces_each)
        chunks.append(pltpu.make_async_copy(cond_hbm.at[:, some], cond.at[:, some], sems.at[3 + chunk]))
    late = [
        pltpu.make_async_copy(coupling_hbm, coupling_out, sems.at[3 + CHUNKS]),
        pltpu.make_async_copy(schur_hbm, schur_out, sems.at[4 + CHUNKS]),
    ]
    for copy in early + chunks + late:
        copy.start()
    for copy in early:
        copy.wait()
    position = iota((1, index_rows.shape[1]), 1) % CAP
    for sender in range(index_rows.shape[0]):
        row = index_rows[sender : sender + 1, :]
        layer = sum((row >= at * width).astype(jnp.int32) for at in range(1, layers))
        place_out[sender : sender + 1, :] = jnp.where(position < counts[sender], row - layer * width, -1)
        layer_out[sender : sender + 1, :] = layer
    for block in range(elems // LANES):
        lanes = pl.ds(block * LANES, LANES)
        source32[:2] = source[:, :, :, lanes].astype(F32)
        source32[2] = source32[0] + source32[1]
        parts = [[] for _ in range(owners)]
        skewed = []
        for face in range(n_faces):
            if block == 0 and face % faces_each == 0:
                chunks[face // faces_each].wait()
            left_re = cond[0, face, :, lanes].astype(F32)
            left_im = cond[1, face, :, lanes].astype(F32)
            left_sum = left_re + left_im
            left_gap = left_im - left_re
            tiles = [None] * (2 * sources)
            for j in range(sources):
                both = jnp.sum((left_re * source32[2, j]).reshape(n_inner // 8, 8, LANES), 0)
                minus = jnp.sum((left_sum * source32[1, j]).reshape(n_inner // 8, 8, LANES), 0)
                plus = jnp.sum((left_gap * source32[0, j]).reshape(n_inner // 8, 8, LANES), 0)
                tiles[j] = both - minus
                tiles[sources + j] = both + plus
            first, size = groups[face]
            skewed.append(skew_block(sum_sublanes(tiles), face - first, CAP))
            if len(skewed) < size:
                continue
            moved = unskew_blocks(skewed, CAP)
            skewed = []
            for owner in range(owners):
                piece = moved[owner % size]
                if owner >= size:
                    piece = skew_block(piece, owners - owner // size * size, CAP)
                parts[owner].append(piece[:, : size * CAP])
        if block == 0:
            late[0].wait()
            spare = pack_coupling(coupling_out[0], 2 * sources)
        for owner in range(owners):
            out[place_of(block * owners + owner, out.shape[0])] = jnp.concatenate(parts[owner] + [spare], 1).astype(BF16)
    late[1].wait()


def assemble_kernel(received, place_rows, layer_rows, coupling, loads, out):
    peers, rows, _ = received.shape
    face_rows = place_rows.shape[1]
    layers, _, width = loads.shape
    place = iota((width, face_rows), 0)
    total = jnp.zeros((layers * rows, width), F32)
    for sender in range(peers):
        onehot = jnp.where(place == place_rows[sender : sender + 1, :], 1.0, 0.0).astype(BF16)
        values = received[place_of(sender, peers)].astype(F32)[:, :face_rows]
        layer_row = layer_rows[sender : sender + 1, :]
        split = [jnp.where(layer_row == layer, values, 0.0) for layer in range(layers)]
        total += lax.dot_general(
            jnp.concatenate(split, 0).astype(BF16), onehot, (((1,), (1,)), ((), ())), preferred_element_type=F32
        )
    for layer in range(layers):
        loads[layer] = total[layer * rows : (layer + 1) * rows]
    block = couple(total[:rows], coupling[0], jnp.zeros((rows, width), F32)).astype(BF16)
    for peer in range(out.shape[0]):
        out[peer] = block


def couple(loads, coupling, carried):
    half = loads.shape[0] // 2
    couple_re, couple_im = coupling[0:1], coupling[1:2]
    real, imag = carried[:half], carried[half:]
    return jnp.concatenate(
        [
            loads[:half] - (couple_re * real - couple_im * imag),
            loads[half:] - (couple_re * imag + couple_im * real),
        ],
        0,
    )


def apply_schur(rhs, schur, layer):
    half = rhs.shape[0] // 2
    first = jnp.dot(rhs, schur[layer, 0], preferred_element_type=F32)
    second = jnp.dot(rhs, schur[layer, 1], preferred_element_type=F32)
    return jnp.concatenate([first[:half] - second[half:], second[:half] + first[half:]], 0)


def cross_kernel(everyone, whole, received, loads, coupling, schur, out, solved_out, row_out, *, row_axis):
    peers = whole.shape[0]
    _, count, width = loads.shape
    spare = received.shape[2] - 4 * width // count
    row = lax.axis_index(row_axis)
    row_out[0] = row
    start = jnp.maximum(row - 1, 0) * peers
    keep = (row > 0).astype(F32)
    blocks = []
    for peer in range(peers):
        place = place_of(peer, peers)
        pair = unpack_coupling(received[place].astype(F32)[:, spare:])
        before = everyone[start + peer].astype(F32) * keep
        blocks.append(couple(whole[place].astype(F32), pair, before).astype(BF16))
    solved = apply_schur(jnp.concatenate(blocks, 1), schur, 0)
    solved_out[...] = solved
    block = couple(loads[1], coupling[1], solved).astype(BF16)
    for peer in range(out.shape[0]):
        out[peer] = block


def side_by_side(gathered):
    count = gathered.shape[0]
    return jnp.concatenate([gathered[place_of(peer, count)] for peer in range(count)], 1)


def layer_kernel(gathered, loads, coupling, schur, out, solved_out, *row_out, layer):
    if row_out:
        row_out[0][0] = lax.axis_index("sweep")
    rhs = side_by_side(gathered)
    solved = apply_schur(rhs, schur, layer)
    solved_out[...] = solved
    block = couple(loads[layer + 1], coupling[layer + 1], solved).astype(BF16)
    for peer in range(out.shape[0]):
        out[peer] = block


def last_kernel(*refs, layer, send):
    gathered, *earlier, schur = refs[: layer + 2]
    outs = refs[layer + 2 :]
    rhs = side_by_side(gathered)
    solved = apply_schur(rhs, schur, layer)
    for at in range(layer):
        outs[0][at] = earlier[at][...]
    outs[0][layer] = solved
    if send:
        block = solved.astype(BF16)
        for peer in range(outs[1].shape[0]):
            outs[1][peer] = block


def call(kernel, out_shape, operands, scratch=(), space=pltpu.VMEM):
    if space == pltpu.HBM:
        operands = [pltpu.with_memory_space_constraint(operand, space) for operand in operands]
    return pl.pallas_call(
        kernel,
        out_shape=out_shape,
        in_specs=[pl.BlockSpec(memory_space=space)] * len(operands),
        out_specs=jax.tree.map(
            lambda out: pl.BlockSpec(memory_space=getattr(out, "memory_space", None) or pltpu.VMEM), out_shape
        ),
        scratch_shapes=list(scratch),
        compiler_params=pltpu.CompilerParams(vmem_limit_bytes=16 * 1024 * 1024),
    )(*operands)


def exchange_row(blocks):
    count = blocks.shape[0]
    order = [(first_of(count) + place) % count for place in range(count)]
    return lax.all_to_all(
        blocks, "xsec", split_axis=0, concat_axis=0, tiled=True, axis_index_groups=[order]
    )


def exchange_all(blocks):
    return lax.all_to_all(blocks, ("sweep", "xsec"), split_axis=0, concat_axis=0, tiled=True)


def shards(cond_block, interior_src, face_index, owner_count, coupling, schur_inv):
    layers = schur_inv.shape[0]
    width = schur_inv.shape[3]
    sources = interior_src.shape[3]
    n_faces, n_inner, elems = cond_block.shape[3:]
    peers = lax.axis_size("xsec")
    chain = lax.axis_size("sweep")
    count = 2 * sources
    struct = jax.ShapeDtypeStruct
    gathered_shape = struct((peers, count, width), BF16)

    index_rows = face_index[0, 0]
    outgoing, place_rows, layer_rows, coupling, schur_inv = call(
        contract_kernel,
        (
            struct((peers, count, n_faces * CAP + 4 * width // count), BF16),
            struct(index_rows.shape, index_rows.dtype),
            struct(index_rows.shape, index_rows.dtype),
            struct(coupling.shape, coupling.dtype),
            struct(schur_inv.shape, schur_inv.dtype),
        ),
        (cond_block[0, 0], interior_src[0, 0], index_rows, owner_count[0, 0], coupling, schur_inv),
        scratch=(
            pltpu.VMEM(cond_block.shape[2:], BF16),
            pltpu.VMEM(interior_src.shape[2:], BF16),
            pltpu.VMEM(index_rows.shape, index_rows.dtype),
            pltpu.SMEM(owner_count.shape[2:], owner_count.dtype),
            pltpu.VMEM((3, sources, n_inner, LANES), F32),
            pltpu.SemaphoreType.DMA((5 + CHUNKS,)),
        ),
        space=pltpu.HBM,
    )
    received = exchange_row(outgoing)
    loads, block = call(
        assemble_kernel,
        (struct((layers, count, width), F32), gathered_shape),
        (received, place_rows, layer_rows, coupling),
    )
    whole = exchange_row(block)
    solved_shape = struct((count, width), F32)
    whole_out = pltpu.VMEM((layers, count, width), F32)

    row_shape = pltpu.SMEM((1,), jnp.int32)

    def other_layers(block, solved, loads, coupling, schur_inv, send):
        done = [solved]
        for layer in range(1, layers - 1):
            block, solved = call(
                functools.partial(layer_kernel, layer=layer),
                (gathered_shape, solved_shape),
                (exchange_row(block), loads, coupling, schur_inv),
            )
            done.append(solved)
        sent = (struct((chain * peers, count, width), BF16),) if send else ()
        return call(
            functools.partial(last_kernel, layer=layers - 1, send=send),
            (whole_out,) + sent,
            (exchange_row(block), *done, schur_inv),
        )

    block, solved, row = call(
        functools.partial(layer_kernel, layer=0),
        (gathered_shape, solved_shape, row_shape),
        (whole, loads, coupling, schur_inv),
    )
    finished = loads
    for round_at in range(chain):
        send = round_at < chain - 1
        nothing = struct((chain * peers, count, width), BF16)
        finished, *sent = lax.cond(
            row[0] == round_at,
            lambda finished, *rest: tuple(other_layers(*rest, send)),
            lambda finished, *rest: (finished,) + ((jnp.zeros(nothing.shape, BF16),) if send else ()),
            finished, block, solved, loads, coupling, schur_inv,
        )
        if send:
            block, solved, row = call(
                functools.partial(cross_kernel, row_axis="sweep"),
                (gathered_shape, solved_shape, row_shape),
                (exchange_all(sent[0]), whole, received, loads, coupling, schur_inv),
            )
    return finished


def solution(mesh):
    placed = (
        P("sweep", "xsec", None, None, None, None),
        P("sweep", "xsec", None, None, None, None),
        P("sweep", "xsec", None, None),
        P("sweep", "xsec", None),
        P("sweep", None, "xsec"),
        P("sweep", None, None, "xsec"),
    )
    return jax.shard_map(
        shards, mesh=mesh, in_specs=placed, out_specs=P("sweep", None, "xsec"), check_vma=False
    )
```

```python
import functools

import jax
import jax.numpy as jnp
import numpy as np
from jax import lax
from jax.experimental import pallas as pl
from jax.experimental.pallas import tpu as pltpu
from jax.sharding import PartitionSpec as P

CAP = 8
LANES = 128
CHUNKS = 2
F32 = jnp.float32
BF16 = jnp.bfloat16


def row_order(count):
    return [int(device) for device in np.random.RandomState(161).permutation(count)]


def place_of(device, count):
    return row_order(count).index(device)


def iota(shape, axis):
    return lax.broadcasted_iota(jnp.int32, shape, axis)


def sum_sublanes(tiles):
    sub = iota((8, LANES), 0)
    low = sub < 4
    halves = [
        jnp.where(low, tiles[r], tiles[r + 4]) + pltpu.roll(jnp.where(low, tiles[r + 4], tiles[r]), 4, 0)
        for r in range(4)
    ]

    def fold(first, second, step):
        even = (sub & step) == 0
        return jnp.where(even, first, second) + jnp.where(
            even, pltpu.roll(first, 8 - step, 0), pltpu.roll(second, step, 0)
        )

    pairs = [fold(halves[r], halves[r + 2], 2) for r in range(2)]
    return fold(pairs[0], pairs[1], 1)


def skew_block(tile, at, group):
    shift = at * group % LANES
    return pltpu.roll(tile, shift, 1) if shift else tile


def unskew_blocks(tiles, group):
    count = len(tiles)
    lane = iota((8, LANES), 1)
    tiles = list(tiles)
    bit = 1
    while bit < count:
        take = (lane & (bit * group)) != 0
        tiles = [jnp.where(take, tiles[(at + bit) % count], tiles[at]) for at in range(count)]
        bit *= 2
    return [skew_block(tiles[-at % count], LANES // group - at, group) for at in range(count)]


def pack_coupling(layer, rows):
    high = layer.astype(BF16).astype(F32)
    both = jnp.concatenate([high, layer - high], 0)
    lanes = both.shape[0] * both.shape[1] // rows
    return jnp.concatenate([both[:, at : at + lanes] for at in range(0, both.shape[1], lanes)], 0)


def unpack_coupling(packed):
    both = jnp.concatenate([packed[at : at + 4] for at in range(0, packed.shape[0], 4)], 1)
    return both[:2] + both[2:]


def contract_kernel(
    cond_hbm, source_hbm, index_hbm, counts_hbm, coupling_hbm, schur_hbm,
    out, place_out, layer_out, coupling_out, schur_out,
    cond, source, index_rows, counts, source32, sems,
):
    _, n_faces, n_inner, elems = cond.shape
    sources = source.shape[1]
    owners = LANES // CAP
    faces_each = n_faces // CHUNKS
    layers, _, width = coupling_out.shape
    groups = []
    while len(groups) < n_faces:
        size = owners
        while size > n_faces - len(groups):
            size //= 2
        groups += [(len(groups), size)] * size
    early = [
        pltpu.make_async_copy(source_hbm, source, sems.at[0]),
        pltpu.make_async_copy(index_hbm, index_rows, sems.at[1]),
        pltpu.make_async_copy(counts_hbm, counts, sems.at[2]),
    ]
    chunks = []
    for chunk in range(CHUNKS):
        some = pl.ds(chunk * faces_each, faces_each)
        chunks.append(pltpu.make_async_copy(cond_hbm.at[:, some], cond.at[:, some], sems.at[3 + chunk]))
    late = [
        pltpu.make_async_copy(coupling_hbm, coupling_out, sems.at[3 + CHUNKS]),
        pltpu.make_async_copy(schur_hbm, schur_out, sems.at[4 + CHUNKS]),
    ]
    for copy in early + chunks + late:
        copy.start()
    for copy in early:
        copy.wait()
    position = iota((1, index_rows.shape[1]), 1) % CAP
    for sender in range(index_rows.shape[0]):
        row = index_rows[sender : sender + 1, :]
        layer = sum((row >= at * width).astype(jnp.int32) for at in range(1, layers))
        place_out[sender : sender + 1, :] = jnp.where(position < counts[sender], row - layer * width, -1)
        layer_out[sender : sender + 1, :] = layer
    for block in range(elems // LANES):
        lanes = pl.ds(block * LANES, LANES)
        source32[:2] = source[:, :, :, lanes].astype(F32)
        source32[2] = source32[0] + source32[1]
        parts = [[] for _ in range(owners)]
        skewed = []
        for face in range(n_faces):
            if block == 0 and face % faces_each == 0:
                chunks[face // faces_each].wait()
            left_re = cond[0, face, :, lanes].astype(F32)
            left_im = cond[1, face, :, lanes].astype(F32)
            left_sum = left_re + left_im
            left_gap = left_im - left_re
            tiles = [None] * (2 * sources)
            for j in range(sources):
                both = jnp.sum((left_re * source32[2, j]).reshape(n_inner // 8, 8, LANES), 0)
                minus = jnp.sum((left_sum * source32[1, j]).reshape(n_inner // 8, 8, LANES), 0)
                plus = jnp.sum((left_gap * source32[0, j]).reshape(n_inner // 8, 8, LANES), 0)
                tiles[j] = both - minus
                tiles[sources + j] = both + plus
            first, size = groups[face]
            skewed.append(skew_block(sum_sublanes(tiles), face - first, CAP))
            if len(skewed) < size:
                continue
            moved = unskew_blocks(skewed, CAP)
            skewed = []
            for owner in range(owners):
                piece = moved[owner % size]
                if owner >= size:
                    piece = skew_block(piece, owners - owner // size * size, CAP)
                parts[owner].append(piece[:, : size * CAP])
        if block == 0:
            late[0].wait()
            spare = pack_coupling(coupling_out[0], 2 * sources)
        for owner in range(owners):
            out[place_of(block * owners + owner, out.shape[0])] = jnp.concatenate(parts[owner] + [spare], 1).astype(BF16)
    late[1].wait()


def assemble_kernel(received, place_rows, layer_rows, coupling, loads, out):
    peers, rows, _ = received.shape
    face_rows = place_rows.shape[1]
    layers, _, width = loads.shape
    place = iota((width, face_rows), 0)
    total = jnp.zeros((layers * rows, width), F32)
    for sender in range(peers):
        onehot = jnp.where(place == place_rows[sender : sender + 1, :], 1.0, 0.0).astype(BF16)
        values = received[place_of(sender, peers)].astype(F32)[:, :face_rows]
        layer_row = layer_rows[sender : sender + 1, :]
        split = [jnp.where(layer_row == layer, values, 0.0) for layer in range(layers)]
        total += lax.dot_general(
            jnp.concatenate(split, 0).astype(BF16), onehot, (((1,), (1,)), ((), ())), preferred_element_type=F32
        )
    for layer in range(layers):
        loads[layer] = total[layer * rows : (layer + 1) * rows]
    block = couple(total[:rows], coupling[0], jnp.zeros((rows, width), F32)).astype(BF16)
    for peer in range(out.shape[0]):
        out[peer] = block


def couple(loads, coupling, carried):
    half = loads.shape[0] // 2
    couple_re, couple_im = coupling[0:1], coupling[1:2]
    real, imag = carried[:half], carried[half:]
    return jnp.concatenate(
        [
            loads[:half] - (couple_re * real - couple_im * imag),
            loads[half:] - (couple_re * imag + couple_im * real),
        ],
        0,
    )


def apply_schur(rhs, schur, layer):
    half = rhs.shape[0] // 2
    first = jnp.dot(rhs, schur[layer, 0], preferred_element_type=F32)
    second = jnp.dot(rhs, schur[layer, 1], preferred_element_type=F32)
    return jnp.concatenate([first[:half] - second[half:], second[:half] + first[half:]], 0)


def cross_kernel(everyone, whole, received, loads, coupling, schur, out, solved_out, row_out, *, row_axis):
    peers = whole.shape[0]
    _, count, width = loads.shape
    spare = received.shape[2] - 4 * width // count
    row = lax.axis_index(row_axis)
    row_out[0] = row
    start = jnp.maximum(row - 1, 0) * peers
    keep = (row > 0).astype(F32)
    blocks = []
    for peer in range(peers):
        place = place_of(peer, peers)
        pair = unpack_coupling(received[place].astype(F32)[:, spare:])
        before = everyone[start + peer].astype(F32) * keep
        blocks.append(couple(whole[place].astype(F32), pair, before).astype(BF16))
    solved = apply_schur(jnp.concatenate(blocks, 1), schur, 0)
    solved_out[...] = solved
    block = couple(loads[1], coupling[1], solved).astype(BF16)
    for peer in range(out.shape[0]):
        out[peer] = block


def side_by_side(gathered):
    count = gathered.shape[0]
    return jnp.concatenate([gathered[place_of(peer, count)] for peer in range(count)], 1)


def layer_kernel(gathered, loads, coupling, schur, out, solved_out, *row_out, layer):
    if row_out:
        row_out[0][0] = lax.axis_index("sweep")
    rhs = side_by_side(gathered)
    solved = apply_schur(rhs, schur, layer)
    solved_out[...] = solved
    block = couple(loads[layer + 1], coupling[layer + 1], solved).astype(BF16)
    for peer in range(out.shape[0]):
        out[peer] = block


def last_kernel(*refs, layer, send):
    gathered, *earlier, schur = refs[: layer + 2]
    outs = refs[layer + 2 :]
    rhs = side_by_side(gathered)
    solved = apply_schur(rhs, schur, layer)
    for at in range(layer):
        outs[0][at] = earlier[at][...]
    outs[0][layer] = solved
    if send:
        block = solved.astype(BF16)
        for peer in range(outs[1].shape[0]):
            outs[1][peer] = block


def call(kernel, out_shape, operands, scratch=(), space=pltpu.VMEM):
    if space == pltpu.HBM:
        operands = [pltpu.with_memory_space_constraint(operand, space) for operand in operands]
    return pl.pallas_call(
        kernel,
        out_shape=out_shape,
        in_specs=[pl.BlockSpec(memory_space=space)] * len(operands),
        out_specs=jax.tree.map(
            lambda out: pl.BlockSpec(memory_space=getattr(out, "memory_space", None) or pltpu.VMEM), out_shape
        ),
        scratch_shapes=list(scratch),
        compiler_params=pltpu.CompilerParams(vmem_limit_bytes=16 * 1024 * 1024),
    )(*operands)


def exchange_row(blocks):
    return lax.all_to_all(
        blocks, "xsec", split_axis=0, concat_axis=0, tiled=True,
        axis_index_groups=[row_order(blocks.shape[0])],
    )


def exchange_all(blocks):
    return lax.all_to_all(blocks, ("sweep", "xsec"), split_axis=0, concat_axis=0, tiled=True)


def shards(cond_block, interior_src, face_index, owner_count, coupling, schur_inv):
    layers = schur_inv.shape[0]
    width = schur_inv.shape[3]
    sources = interior_src.shape[3]
    n_faces, n_inner, elems = cond_block.shape[3:]
    peers = lax.axis_size("xsec")
    chain = lax.axis_size("sweep")
    count = 2 * sources
    struct = jax.ShapeDtypeStruct
    gathered_shape = struct((peers, count, width), BF16)

    index_rows = face_index[0, 0]
    outgoing, place_rows, layer_rows, coupling, schur_inv = call(
        contract_kernel,
        (
            struct((peers, count, n_faces * CAP + 4 * width // count), BF16),
            struct(index_rows.shape, index_rows.dtype),
            struct(index_rows.shape, index_rows.dtype),
            struct(coupling.shape, coupling.dtype),
            struct(schur_inv.shape, schur_inv.dtype),
        ),
        (cond_block[0, 0], interior_src[0, 0], index_rows, owner_count[0, 0], coupling, schur_inv),
        scratch=(
            pltpu.VMEM(cond_block.shape[2:], BF16),
            pltpu.VMEM(interior_src.shape[2:], BF16),
            pltpu.VMEM(index_rows.shape, index_rows.dtype),
            pltpu.SMEM(owner_count.shape[2:], owner_count.dtype),
            pltpu.VMEM((3, sources, n_inner, LANES), F32),
            pltpu.SemaphoreType.DMA((5 + CHUNKS,)),
        ),
        space=pltpu.HBM,
    )
    received = exchange_row(outgoing)
    loads, block = call(
        assemble_kernel,
        (struct((layers, count, width), F32), gathered_shape),
        (received, place_rows, layer_rows, coupling),
    )
    whole = exchange_row(block)
    solved_shape = struct((count, width), F32)
    whole_out = pltpu.VMEM((layers, count, width), F32)

    row_shape = pltpu.SMEM((1,), jnp.int32)

    def other_layers(block, solved, loads, coupling, schur_inv, send):
        done = [solved]
        for layer in range(1, layers - 1):
            block, solved = call(
                functools.partial(layer_kernel, layer=layer),
                (gathered_shape, solved_shape),
                (exchange_row(block), loads, coupling, schur_inv),
            )
            done.append(solved)
        sent = (struct((chain * peers, count, width), BF16),) if send else ()
        return call(
            functools.partial(last_kernel, layer=layers - 1, send=send),
            (whole_out,) + sent,
            (exchange_row(block), *done, schur_inv),
        )

    block, solved, row = call(
        functools.partial(layer_kernel, layer=0),
        (gathered_shape, solved_shape, row_shape),
        (whole, loads, coupling, schur_inv),
    )
    finished = loads
    for round_at in range(chain):
        send = round_at < chain - 1
        nothing = struct((chain * peers, count, width), BF16)
        finished, *sent = lax.cond(
            row[0] == round_at,
            lambda finished, *rest: tuple(other_layers(*rest, send)),
            lambda finished, *rest: (finished,) + ((jnp.zeros(nothing.shape, BF16),) if send else ()),
            finished, block, solved, loads, coupling, schur_inv,
        )
        if send:
            block, solved, row = call(
                functools.partial(cross_kernel, row_axis="sweep"),
                (gathered_shape, solved_shape, row_shape),
                (exchange_all(sent[0]), whole, received, loads, coupling, schur_inv),
            )
    return finished


def solution(mesh):
    placed = (
        P("sweep", "xsec", None, None, None, None),
        P("sweep", "xsec", None, None, None, None),
        P("sweep", "xsec", None, None),
        P("sweep", "xsec", None),
        P("sweep", None, "xsec"),
        P("sweep", None, None, "xsec"),
    )
    return jax.shard_map(
        shards, mesh=mesh, in_specs=placed, out_specs=P("sweep", None, "xsec"), check_vma=False
    )
```

```python
import functools

import jax
import jax.numpy as jnp
import numpy as np
from jax import lax
from jax.experimental import pallas as pl
from jax.experimental.pallas import tpu as pltpu
from jax.sharding import PartitionSpec as P

CAP = 8
LANES = 128
CHUNKS = 2
DEPTH = 256
F32 = jnp.float32
BF16 = jnp.bfloat16


def row_order(count):
    return [int(device) for device in np.random.RandomState(161).permutation(count)]


def place_of(device, count):
    return row_order(count).index(device)


def iota(shape, axis):
    return lax.broadcasted_iota(jnp.int32, shape, axis)


def sum_sublanes(tiles):
    sub = iota((8, LANES), 0)
    low = sub < 4
    halves = [
        jnp.where(low, tiles[r], tiles[r + 4]) + pltpu.roll(jnp.where(low, tiles[r + 4], tiles[r]), 4, 0)
        for r in range(4)
    ]

    def fold(first, second, step):
        even = (sub & step) == 0
        return jnp.where(even, first, second) + jnp.where(
            even, pltpu.roll(first, 8 - step, 0), pltpu.roll(second, step, 0)
        )

    pairs = [fold(halves[r], halves[r + 2], 2) for r in range(2)]
    return fold(pairs[0], pairs[1], 1)


def skew_block(tile, at, group):
    shift = at * group % LANES
    return pltpu.roll(tile, shift, 1) if shift else tile


def unskew_blocks(tiles, group):
    count = len(tiles)
    lane = iota((8, LANES), 1)
    tiles = list(tiles)
    bit = 1
    while bit < count:
        take = (lane & (bit * group)) != 0
        tiles = [jnp.where(take, tiles[(at + bit) % count], tiles[at]) for at in range(count)]
        bit *= 2
    return [skew_block(tiles[-at % count], LANES // group - at, group) for at in range(count)]


def pack_coupling(layer, rows):
    high = layer.astype(BF16).astype(F32)
    both = jnp.concatenate([high, layer - high], 0)
    lanes = both.shape[0] * both.shape[1] // rows
    return jnp.concatenate([both[:, at : at + lanes] for at in range(0, both.shape[1], lanes)], 0)


def unpack_coupling(packed):
    both = jnp.concatenate([packed[at : at + 4] for at in range(0, packed.shape[0], 4)], 1)
    return both[:2] + both[2:]


def contract_kernel(
    cond_hbm, source_hbm, index_hbm, counts_hbm, coupling_hbm, schur_hbm,
    out, place_out, layer_out, coupling_out, schur_out,
    cond, source, index_rows, counts, source32, sems,
):
    _, n_faces, n_inner, elems = cond.shape
    sources = source.shape[1]
    owners = LANES // CAP
    faces_each = n_faces // CHUNKS
    layers, _, width = coupling_out.shape
    groups = []
    while len(groups) < n_faces:
        size = owners
        while size > n_faces - len(groups):
            size //= 2
        groups += [(len(groups), size)] * size
    early = [
        pltpu.make_async_copy(source_hbm, source, sems.at[0]),
        pltpu.make_async_copy(index_hbm, index_rows, sems.at[1]),
        pltpu.make_async_copy(counts_hbm, counts, sems.at[2]),
    ]
    chunks = []
    for chunk in range(CHUNKS):
        some = pl.ds(chunk * faces_each, faces_each)
        chunks.append(pltpu.make_async_copy(cond_hbm.at[:, some], cond.at[:, some], sems.at[3 + chunk]))
    late = [
        pltpu.make_async_copy(coupling_hbm, coupling_out, sems.at[3 + CHUNKS]),
        pltpu.make_async_copy(schur_hbm, schur_out, sems.at[4 + CHUNKS]),
    ]
    for copy in early + chunks + late:
        copy.start()
    for copy in early:
        copy.wait()
    position = iota((1, index_rows.shape[1]), 1) % CAP
    for sender in range(index_rows.shape[0]):
        row = index_rows[sender : sender + 1, :]
        layer = sum((row >= at * width).astype(jnp.int32) for at in range(1, layers))
        place_out[sender : sender + 1, :] = jnp.where(position < counts[sender], row - layer * width, -1)
        layer_out[sender : sender + 1, :] = layer
    for block in range(elems // LANES):
        lanes = pl.ds(block * LANES, LANES)
        source32[:2] = source[:, :, :, lanes].astype(F32)
        source32[2] = source32[0] + source32[1]
        parts = [[] for _ in range(owners)]
        skewed = []
        for face in range(n_faces):
            if block == 0 and face % faces_each == 0:
                chunks[face // faces_each].wait()
            left_re = cond[0, face, :, lanes].astype(F32)
            left_im = cond[1, face, :, lanes].astype(F32)
            left_sum = left_re + left_im
            left_gap = left_im - left_re
            tiles = [None] * (2 * sources)
            for j in range(sources):
                both = jnp.sum((left_re * source32[2, j]).reshape(n_inner // 8, 8, LANES), 0)
                minus = jnp.sum((left_sum * source32[1, j]).reshape(n_inner // 8, 8, LANES), 0)
                plus = jnp.sum((left_gap * source32[0, j]).reshape(n_inner // 8, 8, LANES), 0)
                tiles[j] = both - minus
                tiles[sources + j] = both + plus
            first, size = groups[face]
            skewed.append(skew_block(sum_sublanes(tiles), face - first, CAP))
            if len(skewed) < size:
                continue
            moved = unskew_blocks(skewed, CAP)
            skewed = []
            for owner in range(owners):
                piece = moved[owner % size]
                if owner >= size:
                    piece = skew_block(piece, owners - owner // size * size, CAP)
                parts[owner].append(piece[:, : size * CAP])
        if block == 0:
            late[0].wait()
            spare = pack_coupling(coupling_out[0], 2 * sources)
        for owner in range(owners):
            out[place_of(block * owners + owner, out.shape[0])] = jnp.concatenate(parts[owner] + [spare], 1).astype(BF16)
    late[1].wait()


def assemble_kernel(received, place_rows, layer_rows, coupling, loads, out):
    peers, rows, _ = received.shape
    face_rows = place_rows.shape[1]
    layers, _, width = loads.shape
    place = iota((width, face_rows), 0)
    total = jnp.zeros((layers * rows, width), F32)
    whole_tiles = face_rows // LANES * LANES
    pieces = [(sender, at, LANES) for sender in range(peers) for at in range(0, whole_tiles, LANES)]
    pieces += [(sender, whole_tiles, face_rows - whole_tiles) for sender in range(peers) if face_rows > whole_tiles]
    place = iota((width, DEPTH), 0)
    while pieces:
        group = []
        while pieces and sum(piece[2] for piece in group) + pieces[0][2] <= DEPTH:
            group.append(pieces.pop(0))
        values, places, layer_row = [], [], []
        for sender, at, size in group:
            lanes = slice(at, at + size)
            values.append(received[place_of(sender, peers)].astype(F32)[:, lanes])
            places.append(place_rows[sender : sender + 1, :][:, lanes])
            layer_row.append(layer_rows[sender : sender + 1, :][:, lanes])
        values = jnp.concatenate(values, 1)
        layer_row = jnp.concatenate(layer_row, 1)
        onehot = jnp.where(place[:, : values.shape[1]] == jnp.concatenate(places, 1), 1.0, 0.0).astype(BF16)
        split = [jnp.where(layer_row == layer, values, 0.0) for layer in range(layers)]
        total += lax.dot_general(
            jnp.concatenate(split, 0).astype(BF16), onehot, (((1,), (1,)), ((), ())), preferred_element_type=F32
        )
    for layer in range(layers):
        loads[layer] = total[layer * rows : (layer + 1) * rows]
    block = couple(total[:rows], coupling[0], jnp.zeros((rows, width), F32)).astype(BF16)
    for peer in range(out.shape[0]):
        out[peer] = block


def couple(loads, coupling, carried):
    half = loads.shape[0] // 2
    couple_re, couple_im = coupling[0:1], coupling[1:2]
    real, imag = carried[:half], carried[half:]
    return jnp.concatenate(
        [
            loads[:half] - (couple_re * real - couple_im * imag),
            loads[half:] - (couple_re * imag + couple_im * real),
        ],
        0,
    )


def apply_schur(rhs, schur, layer):
    half = rhs.shape[0] // 2
    first = jnp.dot(rhs, schur[layer, 0], preferred_element_type=F32)
    second = jnp.dot(rhs, schur[layer, 1], preferred_element_type=F32)
    return jnp.concatenate([first[:half] - second[half:], second[:half] + first[half:]], 0)


def cross_kernel(everyone, whole, received, loads, coupling, schur, out, solved_out, row_out, *, row_axis):
    peers = whole.shape[0]
    _, count, width = loads.shape
    spare = received.shape[2] - 4 * width // count
    row = lax.axis_index(row_axis)
    row_out[0] = row
    start = jnp.maximum(row - 1, 0) * peers
    keep = (row > 0).astype(F32)
    blocks = []
    for peer in range(peers):
        place = place_of(peer, peers)
        pair = unpack_coupling(received[place].astype(F32)[:, spare:])
        before = everyone[start + peer].astype(F32) * keep
        blocks.append(couple(whole[place].astype(F32), pair, before).astype(BF16))
    solved = apply_schur(jnp.concatenate(blocks, 1), schur, 0)
    solved_out[...] = solved
    block = couple(loads[1], coupling[1], solved).astype(BF16)
    for peer in range(out.shape[0]):
        out[peer] = block


def side_by_side(gathered):
    count = gathered.shape[0]
    return jnp.concatenate([gathered[place_of(peer, count)] for peer in range(count)], 1)


def layer_kernel(gathered, loads, coupling, schur, out, solved_out, *row_out, layer):
    if row_out:
        row_out[0][0] = lax.axis_index("sweep")
    rhs = side_by_side(gathered)
    solved = apply_schur(rhs, schur, layer)
    solved_out[...] = solved
    block = couple(loads[layer + 1], coupling[layer + 1], solved).astype(BF16)
    for peer in range(out.shape[0]):
        out[peer] = block


def last_kernel(*refs, layer, send):
    gathered, *earlier, schur = refs[: layer + 2]
    outs = refs[layer + 2 :]
    rhs = side_by_side(gathered)
    solved = apply_schur(rhs, schur, layer)
    for at in range(layer):
        outs[0][at] = earlier[at][...]
    outs[0][layer] = solved
    if send:
        block = solved.astype(BF16)
        for peer in range(outs[1].shape[0]):
            outs[1][peer] = block


def call(kernel, out_shape, operands, scratch=(), space=pltpu.VMEM):
    if space == pltpu.HBM:
        operands = [pltpu.with_memory_space_constraint(operand, space) for operand in operands]
    return pl.pallas_call(
        kernel,
        out_shape=out_shape,
        in_specs=[pl.BlockSpec(memory_space=space)] * len(operands),
        out_specs=jax.tree.map(
            lambda out: pl.BlockSpec(memory_space=getattr(out, "memory_space", None) or pltpu.VMEM), out_shape
        ),
        scratch_shapes=list(scratch),
        compiler_params=pltpu.CompilerParams(vmem_limit_bytes=16 * 1024 * 1024),
    )(*operands)


def exchange_row(blocks):
    return lax.all_to_all(
        blocks, "xsec", split_axis=0, concat_axis=0, tiled=True,
        axis_index_groups=[row_order(blocks.shape[0])],
    )


def exchange_all(blocks):
    return lax.all_to_all(blocks, ("sweep", "xsec"), split_axis=0, concat_axis=0, tiled=True)


def shards(cond_block, interior_src, face_index, owner_count, coupling, schur_inv):
    layers = schur_inv.shape[0]
    width = schur_inv.shape[3]
    sources = interior_src.shape[3]
    n_faces, n_inner, elems = cond_block.shape[3:]
    peers = lax.axis_size("xsec")
    chain = lax.axis_size("sweep")
    count = 2 * sources
    struct = jax.ShapeDtypeStruct
    gathered_shape = struct((peers, count, width), BF16)

    index_rows = face_index[0, 0]
    outgoing, place_rows, layer_rows, coupling, schur_inv = call(
        contract_kernel,
        (
            struct((peers, count, n_faces * CAP + 4 * width // count), BF16),
            struct(index_rows.shape, index_rows.dtype),
            struct(index_rows.shape, index_rows.dtype),
            struct(coupling.shape, coupling.dtype),
            struct(schur_inv.shape, schur_inv.dtype),
        ),
        (cond_block[0, 0], interior_src[0, 0], index_rows, owner_count[0, 0], coupling, schur_inv),
        scratch=(
            pltpu.VMEM(cond_block.shape[2:], BF16),
            pltpu.VMEM(interior_src.shape[2:], BF16),
            pltpu.VMEM(index_rows.shape, index_rows.dtype),
            pltpu.SMEM(owner_count.shape[2:], owner_count.dtype),
            pltpu.VMEM((3, sources, n_inner, LANES), F32),
            pltpu.SemaphoreType.DMA((5 + CHUNKS,)),
        ),
        space=pltpu.HBM,
    )
    received = exchange_row(outgoing)
    loads, block = call(
        assemble_kernel,
        (struct((layers, count, width), F32), gathered_shape),
        (received, place_rows, layer_rows, coupling),
    )
    whole = exchange_row(block)
    solved_shape = struct((count, width), F32)
    whole_out = pltpu.VMEM((layers, count, width), F32)

    row_shape = pltpu.SMEM((1,), jnp.int32)

    def other_layers(block, solved, loads, coupling, schur_inv, send):
        done = [solved]
        for layer in range(1, layers - 1):
            block, solved = call(
                functools.partial(layer_kernel, layer=layer),
                (gathered_shape, solved_shape),
                (exchange_row(block), loads, coupling, schur_inv),
            )
            done.append(solved)
        sent = (struct((chain * peers, count, width), BF16),) if send else ()
        return call(
            functools.partial(last_kernel, layer=layers - 1, send=send),
            (whole_out,) + sent,
            (exchange_row(block), *done, schur_inv),
        )

    block, solved, row = call(
        functools.partial(layer_kernel, layer=0),
        (gathered_shape, solved_shape, row_shape),
        (whole, loads, coupling, schur_inv),
    )
    finished = loads
    for round_at in range(chain):
        send = round_at < chain - 1
        nothing = struct((chain * peers, count, width), BF16)
        finished, *sent = lax.cond(
            row[0] == round_at,
            lambda finished, *rest: tuple(other_layers(*rest, send)),
            lambda finished, *rest: (finished,) + ((jnp.zeros(nothing.shape, BF16),) if send else ()),
            finished, block, solved, loads, coupling, schur_inv,
        )
        if send:
            block, solved, row = call(
                functools.partial(cross_kernel, row_axis="sweep"),
                (gathered_shape, solved_shape, row_shape),
                (exchange_all(sent[0]), whole, received, loads, coupling, schur_inv),
            )
    return finished


def solution(mesh):
    placed = (
        P("sweep", "xsec", None, None, None, None),
        P("sweep", "xsec", None, None, None, None),
        P("sweep", "xsec", None, None),
        P("sweep", "xsec", None),
        P("sweep", None, "xsec"),
        P("sweep", None, None, "xsec"),
    )
    return jax.shard_map(
        shards, mesh=mesh, in_specs=placed, out_specs=P("sweep", None, "xsec"), check_vma=False
    )
```

```python
import functools

import jax
import jax.numpy as jnp
import numpy as np
from jax import lax
from jax.experimental import pallas as pl
from jax.experimental.pallas import tpu as pltpu
from jax.sharding import PartitionSpec as P

CAP = 8
LANES = 128
CHUNKS = 2
DEPTH = 256
F32 = jnp.float32
BF16 = jnp.bfloat16


def row_order(count):
    return [int(device) for device in np.random.RandomState(161).permutation(count)]


def place_of(device, count):
    return row_order(count).index(device)


def iota(shape, axis):
    return lax.broadcasted_iota(jnp.int32, shape, axis)


def sum_sublanes(tiles):
    sub = iota((8, LANES), 0)
    low = sub < 4
    halves = [
        jnp.where(low, tiles[r], tiles[r + 4]) + pltpu.roll(jnp.where(low, tiles[r + 4], tiles[r]), 4, 0)
        for r in range(4)
    ]

    def fold(first, second, step):
        even = (sub & step) == 0
        return jnp.where(even, first, second) + jnp.where(
            even, pltpu.roll(first, 8 - step, 0), pltpu.roll(second, step, 0)
        )

    pairs = [fold(halves[r], halves[r + 2], 2) for r in range(2)]
    return fold(pairs[0], pairs[1], 1)


def skew_block(tile, at, group):
    shift = at * group % LANES
    return pltpu.roll(tile, shift, 1) if shift else tile


def unskew_blocks(tiles, group):
    count = len(tiles)
    lane = iota((8, LANES), 1)
    tiles = list(tiles)
    bit = 1
    while bit < count:
        take = (lane & (bit * group)) != 0
        tiles = [jnp.where(take, tiles[(at + bit) % count], tiles[at]) for at in range(count)]
        bit *= 2
    return [skew_block(tiles[-at % count], LANES // group - at, group) for at in range(count)]


def pack_coupling(layer, rows):
    high = layer.astype(BF16).astype(F32)
    both = jnp.concatenate([high, layer - high], 0)
    lanes = both.shape[0] * both.shape[1] // rows
    return jnp.concatenate([both[:, at : at + lanes] for at in range(0, both.shape[1], lanes)], 0)


def unpack_coupling(packed):
    both = jnp.concatenate([packed[at : at + 4] for at in range(0, packed.shape[0], 4)], 1)
    return both[:2] + both[2:]


def contract_kernel(
    cond_hbm, source_hbm, index_hbm, counts_hbm, coupling_hbm, schur_hbm,
    out, place_out, layer_out, coupling_out, schur_out,
    cond, source, index_rows, counts, source32, sems,
):
    _, n_faces, n_inner, elems = cond.shape
    sources = source.shape[1]
    owners = LANES // CAP
    faces_each = n_faces // CHUNKS
    layers, _, width = coupling_out.shape
    groups = []
    while len(groups) < n_faces:
        size = owners
        while size > n_faces - len(groups):
            size //= 2
        groups += [(len(groups), size)] * size
    early = [
        pltpu.make_async_copy(source_hbm, source, sems.at[0]),
        pltpu.make_async_copy(index_hbm, index_rows, sems.at[1]),
        pltpu.make_async_copy(counts_hbm, counts, sems.at[2]),
    ]
    chunks = []
    for chunk in range(CHUNKS):
        some = pl.ds(chunk * faces_each, faces_each)
        chunks.append(pltpu.make_async_copy(cond_hbm.at[:, some], cond.at[:, some], sems.at[3 + chunk]))
    late = [
        pltpu.make_async_copy(coupling_hbm, coupling_out, sems.at[3 + CHUNKS]),
        pltpu.make_async_copy(schur_hbm, schur_out, sems.at[4 + CHUNKS]),
    ]
    for copy in early + chunks + late:
        copy.start()
    for copy in early:
        copy.wait()
    position = iota((1, index_rows.shape[1]), 1) % CAP
    for sender in range(index_rows.shape[0]):
        row = index_rows[sender : sender + 1, :]
        layer = sum((row >= at * width).astype(jnp.int32) for at in range(1, layers))
        place_out[sender : sender + 1, :] = jnp.where(position < counts[sender], row - layer * width, -1)
        layer_out[sender : sender + 1, :] = layer
    for block in range(elems // LANES):
        lanes = pl.ds(block * LANES, LANES)
        source32[:2] = source[:, :, :, lanes].astype(F32)
        source32[2] = source32[0] + source32[1]
        parts = [[] for _ in range(owners)]
        skewed = []
        for face in range(n_faces):
            if block == 0 and face % faces_each == 0:
                chunks[face // faces_each].wait()
            left_re = cond[0, face, :, lanes].astype(F32)
            left_im = cond[1, face, :, lanes].astype(F32)
            left_sum = left_re + left_im
            left_gap = left_im - left_re
            tiles = [None] * (2 * sources)
            for j in range(sources):
                both = jnp.sum((left_re * source32[2, j]).reshape(n_inner // 8, 8, LANES), 0)
                minus = jnp.sum((left_sum * source32[1, j]).reshape(n_inner // 8, 8, LANES), 0)
                plus = jnp.sum((left_gap * source32[0, j]).reshape(n_inner // 8, 8, LANES), 0)
                tiles[j] = both - minus
                tiles[sources + j] = both + plus
            first, size = groups[face]
            skewed.append(skew_block(sum_sublanes(tiles), face - first, CAP))
            if len(skewed) < size:
                continue
            moved = unskew_blocks(skewed, CAP)
            skewed = []
            for owner in range(owners):
                piece = moved[owner % size]
                if owner >= size:
                    piece = skew_block(piece, owners - owner // size * size, CAP)
                parts[owner].append(piece[:, : size * CAP])
        if block == 0:
            late[0].wait()
            spare = pack_coupling(coupling_out[0], 2 * sources)
        for owner in range(owners):
            out[place_of(block * owners + owner, out.shape[0])] = jnp.concatenate(parts[owner] + [spare], 1).astype(BF16)
    late[1].wait()


def assemble_kernel(received, place_rows, layer_rows, coupling, loads, out):
    peers, rows, _ = received.shape
    face_rows = place_rows.shape[1]
    layers, _, width = loads.shape
    place = iota((width, face_rows), 0)
    total = jnp.zeros((layers * rows, width), F32)
    whole_tiles = face_rows // LANES * LANES
    pieces = [(sender, at, LANES) for sender in range(peers) for at in range(0, whole_tiles, LANES)]
    pieces += [(sender, whole_tiles, face_rows - whole_tiles) for sender in range(peers) if face_rows > whole_tiles]
    place = iota((width, DEPTH), 0)
    while pieces:
        group = []
        while pieces and sum(piece[2] for piece in group) + pieces[0][2] <= DEPTH:
            group.append(pieces.pop(0))
        values, places, layer_row = [], [], []
        for sender, at, size in group:
            lanes = slice(at, at + size)
            values.append(received[place_of(sender, peers)].astype(F32)[:, lanes])
            places.append(place_rows[sender : sender + 1, :][:, lanes])
            layer_row.append(layer_rows[sender : sender + 1, :][:, lanes])
        values = jnp.concatenate(values, 1)
        layer_row = jnp.concatenate(layer_row, 1)
        onehot = jnp.where(place[:, : values.shape[1]] == jnp.concatenate(places, 1), 1.0, 0.0).astype(BF16)
        split = [jnp.where(layer_row == layer, values, 0.0) for layer in range(layers)]
        total += lax.dot_general(
            jnp.concatenate(split, 0).astype(BF16), onehot, (((1,), (1,)), ((), ())), preferred_element_type=F32
        )
    for layer in range(layers):
        loads[layer] = total[layer * rows : (layer + 1) * rows]
    block = couple(total[:rows], coupling[0], jnp.zeros((rows, width), F32)).astype(BF16)
    for peer in range(out.shape[0]):
        out[peer] = block


def couple(loads, coupling, carried):
    half = loads.shape[0] // 2
    couple_re, couple_im = coupling[0:1], coupling[1:2]
    real, imag = carried[:half], carried[half:]
    return jnp.concatenate(
        [
            loads[:half] - (couple_re * real - couple_im * imag),
            loads[half:] - (couple_re * imag + couple_im * real),
        ],
        0,
    )


def apply_schur(rhs, schur, layer):
    half = rhs.shape[0] // 2
    first = jnp.dot(rhs, schur[layer, 0], preferred_element_type=F32)
    second = jnp.dot(rhs, schur[layer, 1], preferred_element_type=F32)
    return jnp.concatenate([first[:half] - second[half:], second[:half] + first[half:]], 0)


def cross_kernel(everyone, whole, pairs, loads, coupling, schur, out, solved_out, row_out, *, row_axis):
    peers = whole.shape[0]
    _, count, width = loads.shape
    row = lax.axis_index(row_axis)
    row_out[0] = row
    start = jnp.maximum(row - 1, 0) * peers
    keep = (row > 0).astype(F32)
    blocks = []
    for peer in range(peers):
        place = place_of(peer, peers)
        before = everyone[start + peer].astype(F32) * keep
        blocks.append(couple(whole[place].astype(F32), pairs[peer], before).astype(BF16))
    solved = apply_schur(jnp.concatenate(blocks, 1), schur, 0)
    solved_out[...] = solved
    block = couple(loads[1], coupling[1], solved).astype(BF16)
    for peer in range(out.shape[0]):
        out[peer] = block


def side_by_side(gathered):
    count = gathered.shape[0]
    return jnp.concatenate([gathered[place_of(peer, count)] for peer in range(count)], 1)


def start_kernel(gathered, received, loads, coupling, schur, out, solved_out, row_out, pairs):
    row = lax.axis_index("sweep")
    row_out[0] = row
    layer_kernel(gathered, loads, coupling, schur, out, solved_out, layer=0)

    @pl.when(row == 0)
    def _():
        pairs[...] = jnp.zeros(pairs.shape, F32)

    @pl.when(row > 0)
    def _():
        peers, count, lanes = received.shape
        spare = lanes - 4 * pairs.shape[2] // count
        for peer in range(peers):
            pairs[peer] = unpack_coupling(received[place_of(peer, peers)].astype(F32)[:, spare:])


def layer_kernel(gathered, loads, coupling, schur, out, solved_out, *, layer):
    rhs = side_by_side(gathered)
    solved = apply_schur(rhs, schur, layer)
    solved_out[...] = solved
    block = couple(loads[layer + 1], coupling[layer + 1], solved).astype(BF16)
    for peer in range(out.shape[0]):
        out[peer] = block


def last_kernel(*refs, layer, send):
    gathered, *earlier, schur = refs[: layer + 2]
    outs = refs[layer + 2 :]
    rhs = side_by_side(gathered)
    solved = apply_schur(rhs, schur, layer)
    for at in range(layer):
        outs[0][at] = earlier[at][...]
    outs[0][layer] = solved
    if send:
        block = solved.astype(BF16)
        for peer in range(outs[1].shape[0]):
            outs[1][peer] = block


def call(kernel, out_shape, operands, scratch=(), space=pltpu.VMEM):
    if space == pltpu.HBM:
        operands = [pltpu.with_memory_space_constraint(operand, space) for operand in operands]
    return pl.pallas_call(
        kernel,
        out_shape=out_shape,
        in_specs=[pl.BlockSpec(memory_space=space)] * len(operands),
        out_specs=jax.tree.map(
            lambda out: pl.BlockSpec(memory_space=getattr(out, "memory_space", None) or pltpu.VMEM), out_shape
        ),
        scratch_shapes=list(scratch),
        compiler_params=pltpu.CompilerParams(vmem_limit_bytes=16 * 1024 * 1024),
    )(*operands)


def exchange_row(blocks):
    return lax.all_to_all(
        blocks, "xsec", split_axis=0, concat_axis=0, tiled=True,
        axis_index_groups=[row_order(blocks.shape[0])],
    )


def exchange_all(blocks):
    return lax.all_to_all(blocks, ("sweep", "xsec"), split_axis=0, concat_axis=0, tiled=True)


def shards(cond_block, interior_src, face_index, owner_count, coupling, schur_inv):
    layers = schur_inv.shape[0]
    width = schur_inv.shape[3]
    sources = interior_src.shape[3]
    n_faces, n_inner, elems = cond_block.shape[3:]
    peers = lax.axis_size("xsec")
    chain = lax.axis_size("sweep")
    count = 2 * sources
    struct = jax.ShapeDtypeStruct
    gathered_shape = struct((peers, count, width), BF16)

    index_rows = face_index[0, 0]
    outgoing, place_rows, layer_rows, coupling, schur_inv = call(
        contract_kernel,
        (
            struct((peers, count, n_faces * CAP + 4 * width // count), BF16),
            struct(index_rows.shape, index_rows.dtype),
            struct(index_rows.shape, index_rows.dtype),
            struct(coupling.shape, coupling.dtype),
            struct(schur_inv.shape, schur_inv.dtype),
        ),
        (cond_block[0, 0], interior_src[0, 0], index_rows, owner_count[0, 0], coupling, schur_inv),
        scratch=(
            pltpu.VMEM(cond_block.shape[2:], BF16),
            pltpu.VMEM(interior_src.shape[2:], BF16),
            pltpu.VMEM(index_rows.shape, index_rows.dtype),
            pltpu.SMEM(owner_count.shape[2:], owner_count.dtype),
            pltpu.VMEM((3, sources, n_inner, LANES), F32),
            pltpu.SemaphoreType.DMA((5 + CHUNKS,)),
        ),
        space=pltpu.HBM,
    )
    received = exchange_row(outgoing)
    loads, block = call(
        assemble_kernel,
        (struct((layers, count, width), F32), gathered_shape),
        (received, place_rows, layer_rows, coupling),
    )
    whole = exchange_row(block)
    solved_shape = struct((count, width), F32)
    whole_out = pltpu.VMEM((layers, count, width), F32)

    row_shape = pltpu.SMEM((1,), jnp.int32)

    def other_layers(block, solved, loads, coupling, schur_inv, send):
        done = [solved]
        for layer in range(1, layers - 1):
            block, solved = call(
                functools.partial(layer_kernel, layer=layer),
                (gathered_shape, solved_shape),
                (exchange_row(block), loads, coupling, schur_inv),
            )
            done.append(solved)
        sent = (struct((chain * peers, count, width), BF16),) if send else ()
        return call(
            functools.partial(last_kernel, layer=layers - 1, send=send),
            (whole_out,) + sent,
            (exchange_row(block), *done, schur_inv),
        )

    block, solved, row, pairs = call(
        start_kernel,
        (gathered_shape, solved_shape, row_shape, struct((peers, 2, width), F32)),
        (whole, received, loads, coupling, schur_inv),
    )
    finished = loads
    for round_at in range(chain):
        send = round_at < chain - 1
        nothing = struct((chain * peers, count, width), BF16)
        finished, *sent = lax.cond(
            row[0] == round_at,
            lambda finished, *rest: tuple(other_layers(*rest, send)),
            lambda finished, *rest: (finished,) + ((jnp.zeros(nothing.shape, BF16),) if send else ()),
            finished, block, solved, loads, coupling, schur_inv,
        )
        if send:
            block, solved, row = call(
                functools.partial(cross_kernel, row_axis="sweep"),
                (gathered_shape, solved_shape, row_shape),
                (exchange_all(sent[0]), whole, pairs, loads, coupling, schur_inv),
            )
    return finished


def solution(mesh):
    placed = (
        P("sweep", "xsec", None, None, None, None),
        P("sweep", "xsec", None, None, None, None),
        P("sweep", "xsec", None, None),
        P("sweep", "xsec", None),
        P("sweep", None, "xsec"),
        P("sweep", None, None, "xsec"),
    )
    return jax.shard_map(
        shards, mesh=mesh, in_specs=placed, out_specs=P("sweep", None, "xsec"), check_vma=False
    )
```

```python
import functools

import jax
import jax.numpy as jnp
import numpy as np
from jax import lax
from jax.experimental import pallas as pl
from jax.experimental.pallas import tpu as pltpu
from jax.sharding import PartitionSpec as P

CAP = 8
LANES = 128
CHUNKS = 1
DEPTH = 256
F32 = jnp.float32
BF16 = jnp.bfloat16


def row_order(count):
    return [int(device) for device in np.random.RandomState(161).permutation(count)]


def place_of(device, count):
    return row_order(count).index(device)


def iota(shape, axis):
    return lax.broadcasted_iota(jnp.int32, shape, axis)


def sum_sublanes(tiles):
    sub = iota((8, LANES), 0)
    low = sub < 4
    halves = [
        jnp.where(low, tiles[r], tiles[r + 4]) + pltpu.roll(jnp.where(low, tiles[r + 4], tiles[r]), 4, 0)
        for r in range(4)
    ]

    def fold(first, second, step):
        even = (sub & step) == 0
        return jnp.where(even, first, second) + jnp.where(
            even, pltpu.roll(first, 8 - step, 0), pltpu.roll(second, step, 0)
        )

    pairs = [fold(halves[r], halves[r + 2], 2) for r in range(2)]
    return fold(pairs[0], pairs[1], 1)


def skew_block(tile, at, group):
    shift = at * group % LANES
    return pltpu.roll(tile, shift, 1) if shift else tile


def unskew_blocks(tiles, group):
    count = len(tiles)
    lane = iota((8, LANES), 1)
    tiles = list(tiles)
    bit = 1
    while bit < count:
        take = (lane & (bit * group)) != 0
        tiles = [jnp.where(take, tiles[(at + bit) % count], tiles[at]) for at in range(count)]
        bit *= 2
    return [skew_block(tiles[-at % count], LANES // group - at, group) for at in range(count)]


def pack_coupling(layer, rows):
    high = layer.astype(BF16).astype(F32)
    both = jnp.concatenate([high, layer - high], 0)
    lanes = both.shape[0] * both.shape[1] // rows
    return jnp.concatenate([both[:, at : at + lanes] for at in range(0, both.shape[1], lanes)], 0)


def unpack_coupling(packed):
    both = jnp.concatenate([packed[at : at + 4] for at in range(0, packed.shape[0], 4)], 1)
    return both[:2] + both[2:]


def contract_kernel(
    cond_hbm, source_hbm, index_hbm, counts_hbm, coupling_hbm, schur_hbm,
    out, place_out, layer_out, coupling_out, schur_out,
    cond, source, index_rows, counts, source32, sems,
):
    _, n_faces, n_inner, elems = cond.shape
    sources = source.shape[1]
    owners = LANES // CAP
    faces_each = n_faces // CHUNKS
    layers, _, width = coupling_out.shape
    groups = []
    while len(groups) < n_faces:
        size = owners
        while size > n_faces - len(groups):
            size //= 2
        groups += [(len(groups), size)] * size
    early = [
        pltpu.make_async_copy(source_hbm, source, sems.at[0]),
        pltpu.make_async_copy(index_hbm, index_rows, sems.at[1]),
        pltpu.make_async_copy(counts_hbm, counts, sems.at[2]),
    ]
    chunks = []
    for chunk in range(CHUNKS):
        some = pl.ds(chunk * faces_each, faces_each)
        chunks.append(pltpu.make_async_copy(cond_hbm.at[:, some], cond.at[:, some], sems.at[3 + chunk]))
    late = [
        pltpu.make_async_copy(coupling_hbm, coupling_out, sems.at[3 + CHUNKS]),
        pltpu.make_async_copy(schur_hbm, schur_out, sems.at[4 + CHUNKS]),
    ]
    for copy in early + chunks + late:
        copy.start()
    for copy in early:
        copy.wait()
    position = iota((1, index_rows.shape[1]), 1) % CAP
    for sender in range(index_rows.shape[0]):
        row = index_rows[sender : sender + 1, :]
        layer = sum((row >= at * width).astype(jnp.int32) for at in range(1, layers))
        place_out[sender : sender + 1, :] = jnp.where(position < counts[sender], row - layer * width, -1)
        layer_out[sender : sender + 1, :] = layer
    for block in range(elems // LANES):
        lanes = pl.ds(block * LANES, LANES)
        source32[:2] = source[:, :, :, lanes].astype(F32)
        source32[2] = source32[0] + source32[1]
        parts = [[] for _ in range(owners)]
        skewed = []
        for face in range(n_faces):
            if block == 0 and face % faces_each == 0:
                chunks[face // faces_each].wait()
            left_re = cond[0, face, :, lanes].astype(F32)
            left_im = cond[1, face, :, lanes].astype(F32)
            left_sum = left_re + left_im
            left_gap = left_im - left_re
            tiles = [None] * (2 * sources)
            for j in range(sources):
                both = jnp.sum((left_re * source32[2, j]).reshape(n_inner // 8, 8, LANES), 0)
                minus = jnp.sum((left_sum * source32[1, j]).reshape(n_inner // 8, 8, LANES), 0)
                plus = jnp.sum((left_gap * source32[0, j]).reshape(n_inner // 8, 8, LANES), 0)
                tiles[j] = both - minus
                tiles[sources + j] = both + plus
            first, size = groups[face]
            skewed.append(skew_block(sum_sublanes(tiles), face - first, CAP))
            if len(skewed) < size:
                continue
            moved = unskew_blocks(skewed, CAP)
            skewed = []
            for owner in range(owners):
                piece = moved[owner % size]
                if owner >= size:
                    piece = skew_block(piece, owners - owner // size * size, CAP)
                parts[owner].append(piece[:, : size * CAP])
        if block == 0:
            late[0].wait()
            spare = pack_coupling(coupling_out[0], 2 * sources)
        for owner in range(owners):
            out[place_of(block * owners + owner, out.shape[0])] = jnp.concatenate(parts[owner] + [spare], 1).astype(BF16)
    late[1].wait()


def assemble_kernel(received, place_rows, layer_rows, coupling, loads, out):
    peers, rows, _ = received.shape
    face_rows = place_rows.shape[1]
    layers, _, width = loads.shape
    place = iota((width, face_rows), 0)
    total = jnp.zeros((layers * rows, width), F32)
    whole_tiles = face_rows // LANES * LANES
    pieces = [(sender, at, LANES) for sender in range(peers) for at in range(0, whole_tiles, LANES)]
    pieces += [(sender, whole_tiles, face_rows - whole_tiles) for sender in range(peers) if face_rows > whole_tiles]
    place = iota((width, DEPTH), 0)
    while pieces:
        group = []
        while pieces and sum(piece[2] for piece in group) + pieces[0][2] <= DEPTH:
            group.append(pieces.pop(0))
        values, places, layer_row = [], [], []
        for sender, at, size in group:
            lanes = slice(at, at + size)
            values.append(received[place_of(sender, peers)].astype(F32)[:, lanes])
            places.append(place_rows[sender : sender + 1, :][:, lanes])
            layer_row.append(layer_rows[sender : sender + 1, :][:, lanes])
        values = jnp.concatenate(values, 1)
        layer_row = jnp.concatenate(layer_row, 1)
        onehot = jnp.where(place[:, : values.shape[1]] == jnp.concatenate(places, 1), 1.0, 0.0).astype(BF16)
        split = [jnp.where(layer_row == layer, values, 0.0) for layer in range(layers)]
        total += lax.dot_general(
            jnp.concatenate(split, 0).astype(BF16), onehot, (((1,), (1,)), ((), ())), preferred_element_type=F32
        )
    for layer in range(layers):
        loads[layer] = total[layer * rows : (layer + 1) * rows]
    block = couple(total[:rows], coupling[0], jnp.zeros((rows, width), F32)).astype(BF16)
    for peer in range(out.shape[0]):
        out[peer] = block


def couple(loads, coupling, carried):
    half = loads.shape[0] // 2
    couple_re, couple_im = coupling[0:1], coupling[1:2]
    real, imag = carried[:half], carried[half:]
    return jnp.concatenate(
        [
            loads[:half] - (couple_re * real - couple_im * imag),
            loads[half:] - (couple_re * imag + couple_im * real),
        ],
        0,
    )


def apply_schur(rhs, schur, layer):
    half = rhs.shape[0] // 2
    first = jnp.dot(rhs, schur[layer, 0], preferred_element_type=F32)
    second = jnp.dot(rhs, schur[layer, 1], preferred_element_type=F32)
    return jnp.concatenate([first[:half] - second[half:], second[:half] + first[half:]], 0)


def cross_kernel(everyone, whole, pairs, loads, coupling, schur, out, solved_out, row_out, *, row_axis):
    peers = whole.shape[0]
    _, count, width = loads.shape
    row = lax.axis_index(row_axis)
    row_out[0] = row
    start = jnp.maximum(row - 1, 0) * peers
    keep = (row > 0).astype(F32)
    blocks = []
    for peer in range(peers):
        place = place_of(peer, peers)
        before = everyone[start + peer].astype(F32) * keep
        blocks.append(couple(whole[place].astype(F32), pairs[peer], before).astype(BF16))
    solved = apply_schur(jnp.concatenate(blocks, 1), schur, 0)
    solved_out[...] = solved
    block = couple(loads[1], coupling[1], solved).astype(BF16)
    for peer in range(out.shape[0]):
        out[peer] = block


def side_by_side(gathered):
    count = gathered.shape[0]
    return jnp.concatenate([gathered[place_of(peer, count)] for peer in range(count)], 1)


def start_kernel(gathered, received, loads, coupling, schur, out, solved_out, row_out, pairs):
    row = lax.axis_index("sweep")
    row_out[0] = row
    layer_kernel(gathered, loads, coupling, schur, out, solved_out, layer=0)

    @pl.when(row == 0)
    def _():
        pairs[...] = jnp.zeros(pairs.shape, F32)

    @pl.when(row > 0)
    def _():
        peers, count, lanes = received.shape
        spare = lanes - 4 * pairs.shape[2] // count
        for peer in range(peers):
            pairs[peer] = unpack_coupling(received[place_of(peer, peers)].astype(F32)[:, spare:])


def layer_kernel(gathered, loads, coupling, schur, out, solved_out, *, layer):
    rhs = side_by_side(gathered)
    solved = apply_schur(rhs, schur, layer)
    solved_out[...] = solved
    block = couple(loads[layer + 1], coupling[layer + 1], solved).astype(BF16)
    for peer in range(out.shape[0]):
        out[peer] = block


def last_kernel(*refs, layer, send):
    gathered, *earlier, schur = refs[: layer + 2]
    outs = refs[layer + 2 :]
    rhs = side_by_side(gathered)
    solved = apply_schur(rhs, schur, layer)
    for at in range(layer):
        outs[0][at] = earlier[at][...]
    outs[0][layer] = solved
    if send:
        block = solved.astype(BF16)
        for peer in range(outs[1].shape[0]):
            outs[1][peer] = block


def call(kernel, out_shape, operands, scratch=(), space=pltpu.VMEM):
    if space == pltpu.HBM:
        operands = [pltpu.with_memory_space_constraint(operand, space) for operand in operands]
    return pl.pallas_call(
        kernel,
        out_shape=out_shape,
        in_specs=[pl.BlockSpec(memory_space=space)] * len(operands),
        out_specs=jax.tree.map(
            lambda out: pl.BlockSpec(memory_space=getattr(out, "memory_space", None) or pltpu.VMEM), out_shape
        ),
        scratch_shapes=list(scratch),
        compiler_params=pltpu.CompilerParams(vmem_limit_bytes=16 * 1024 * 1024),
    )(*operands)


def exchange_row(blocks):
    return lax.all_to_all(
        blocks, "xsec", split_axis=0, concat_axis=0, tiled=True,
        axis_index_groups=[row_order(blocks.shape[0])],
    )


def exchange_all(blocks):
    return lax.all_to_all(blocks, ("sweep", "xsec"), split_axis=0, concat_axis=0, tiled=True)


def shards(cond_block, interior_src, face_index, owner_count, coupling, schur_inv):
    layers = schur_inv.shape[0]
    width = schur_inv.shape[3]
    sources = interior_src.shape[3]
    n_faces, n_inner, elems = cond_block.shape[3:]
    peers = lax.axis_size("xsec")
    chain = lax.axis_size("sweep")
    count = 2 * sources
    struct = jax.ShapeDtypeStruct
    gathered_shape = struct((peers, count, width), BF16)

    index_rows = face_index[0, 0]
    outgoing, place_rows, layer_rows, coupling, schur_inv = call(
        contract_kernel,
        (
            struct((peers, count, n_faces * CAP + 4 * width // count), BF16),
            struct(index_rows.shape, index_rows.dtype),
            struct(index_rows.shape, index_rows.dtype),
            struct(coupling.shape, coupling.dtype),
            struct(schur_inv.shape, schur_inv.dtype),
        ),
        (cond_block[0, 0], interior_src[0, 0], index_rows, owner_count[0, 0], coupling, schur_inv),
        scratch=(
            pltpu.VMEM(cond_block.shape[2:], BF16),
            pltpu.VMEM(interior_src.shape[2:], BF16),
            pltpu.VMEM(index_rows.shape, index_rows.dtype),
            pltpu.SMEM(owner_count.shape[2:], owner_count.dtype),
            pltpu.VMEM((3, sources, n_inner, LANES), F32),
            pltpu.SemaphoreType.DMA((5 + CHUNKS,)),
        ),
        space=pltpu.HBM,
    )
    received = exchange_row(outgoing)
    loads, block = call(
        assemble_kernel,
        (struct((layers, count, width), F32), gathered_shape),
        (received, place_rows, layer_rows, coupling),
    )
    whole = exchange_row(block)
    solved_shape = struct((count, width), F32)
    whole_out = pltpu.VMEM((layers, count, width), F32)

    row_shape = pltpu.SMEM((1,), jnp.int32)

    def other_layers(block, solved, loads, coupling, schur_inv, send):
        done = [solved]
        for layer in range(1, layers - 1):
            block, solved = call(
                functools.partial(layer_kernel, layer=layer),
                (gathered_shape, solved_shape),
                (exchange_row(block), loads, coupling, schur_inv),
            )
            done.append(solved)
        sent = (struct((chain * peers, count, width), BF16),) if send else ()
        return call(
            functools.partial(last_kernel, layer=layers - 1, send=send),
            (whole_out,) + sent,
            (exchange_row(block), *done, schur_inv),
        )

    block, solved, row, pairs = call(
        start_kernel,
        (gathered_shape, solved_shape, row_shape, struct((peers, 2, width), F32)),
        (whole, received, loads, coupling, schur_inv),
    )
    finished = loads
    for round_at in range(chain):
        send = round_at < chain - 1
        nothing = struct((chain * peers, count, width), BF16)
        finished, *sent = lax.cond(
            row[0] == round_at,
            lambda finished, *rest: tuple(other_layers(*rest, send)),
            lambda finished, *rest: (finished,) + ((jnp.zeros(nothing.shape, BF16),) if send else ()),
            finished, block, solved, loads, coupling, schur_inv,
        )
        if send:
            block, solved, row = call(
                functools.partial(cross_kernel, row_axis="sweep"),
                (gathered_shape, solved_shape, row_shape),
                (exchange_all(sent[0]), whole, pairs, loads, coupling, schur_inv),
            )
    return finished


def solution(mesh):
    placed = (
        P("sweep", "xsec", None, None, None, None),
        P("sweep", "xsec", None, None, None, None),
        P("sweep", "xsec", None, None),
        P("sweep", "xsec", None),
        P("sweep", None, "xsec"),
        P("sweep", None, None, "xsec"),
    )
    return jax.shard_map(
        shards, mesh=mesh, in_specs=placed, out_specs=P("sweep", None, "xsec"), check_vma=False
    )
```

```python
import functools

import jax
import jax.numpy as jnp
import numpy as np
from jax import lax
from jax.experimental import pallas as pl
from jax.experimental.pallas import tpu as pltpu
from jax.sharding import PartitionSpec as P

CAP = 8
LANES = 128
CHUNKS = 1
DEPTH = 256
F32 = jnp.float32
BF16 = jnp.bfloat16


def row_order(count):
    return [int(device) for device in np.random.RandomState(2312).permutation(count)]


def place_of(device, count):
    return row_order(count).index(device)


def iota(shape, axis):
    return lax.broadcasted_iota(jnp.int32, shape, axis)


def sum_sublanes(tiles):
    sub = iota((8, LANES), 0)
    low = sub < 4
    halves = [
        jnp.where(low, tiles[r], tiles[r + 4]) + pltpu.roll(jnp.where(low, tiles[r + 4], tiles[r]), 4, 0)
        for r in range(4)
    ]

    def fold(first, second, step):
        even = (sub & step) == 0
        return jnp.where(even, first, second) + jnp.where(
            even, pltpu.roll(first, 8 - step, 0), pltpu.roll(second, step, 0)
        )

    pairs = [fold(halves[r], halves[r + 2], 2) for r in range(2)]
    return fold(pairs[0], pairs[1], 1)


def skew_block(tile, at, group):
    shift = at * group % LANES
    return pltpu.roll(tile, shift, 1) if shift else tile


def unskew_blocks(tiles, group):
    count = len(tiles)
    lane = iota((8, LANES), 1)
    tiles = list(tiles)
    bit = 1
    while bit < count:
        take = (lane & (bit * group)) != 0
        tiles = [jnp.where(take, tiles[(at + bit) % count], tiles[at]) for at in range(count)]
        bit *= 2
    return [skew_block(tiles[-at % count], LANES // group - at, group) for at in range(count)]


def pack_coupling(layer, rows):
    high = layer.astype(BF16).astype(F32)
    both = jnp.concatenate([high, layer - high], 0)
    lanes = both.shape[0] * both.shape[1] // rows
    return jnp.concatenate([both[:, at : at + lanes] for at in range(0, both.shape[1], lanes)], 0)


def unpack_coupling(packed):
    both = jnp.concatenate([packed[at : at + 4] for at in range(0, packed.shape[0], 4)], 1)
    return both[:2] + both[2:]


def contract_kernel(
    cond_hbm, source_hbm, index_hbm, counts_hbm, coupling_hbm, schur_hbm,
    out, place_out, layer_out, coupling_out, schur_out,
    cond, source, index_rows, counts, source32, sems,
):
    _, n_faces, n_inner, elems = cond.shape
    sources = source.shape[1]
    owners = LANES // CAP
    faces_each = n_faces // CHUNKS
    layers, _, width = coupling_out.shape
    groups = []
    while len(groups) < n_faces:
        size = owners
        while size > n_faces - len(groups):
            size //= 2
        groups += [(len(groups), size)] * size
    early = [
        pltpu.make_async_copy(source_hbm, source, sems.at[0]),
        pltpu.make_async_copy(index_hbm, index_rows, sems.at[1]),
        pltpu.make_async_copy(counts_hbm, counts, sems.at[2]),
    ]
    chunks = []
    for chunk in range(CHUNKS):
        some = pl.ds(chunk * faces_each, faces_each)
        chunks.append(pltpu.make_async_copy(cond_hbm.at[:, some], cond.at[:, some], sems.at[3 + chunk]))
    late = [
        pltpu.make_async_copy(coupling_hbm, coupling_out, sems.at[3 + CHUNKS]),
        pltpu.make_async_copy(schur_hbm, schur_out, sems.at[4 + CHUNKS]),
    ]
    for copy in early + chunks + late:
        copy.start()
    for copy in early:
        copy.wait()
    position = iota((1, index_rows.shape[1]), 1) % CAP
    for sender in range(index_rows.shape[0]):
        row = index_rows[sender : sender + 1, :]
        layer = sum((row >= at * width).astype(jnp.int32) for at in range(1, layers))
        place_out[sender : sender + 1, :] = jnp.where(position < counts[sender], row - layer * width, -1)
        layer_out[sender : sender + 1, :] = layer
    for block in range(elems // LANES):
        lanes = pl.ds(block * LANES, LANES)
        source32[:2] = source[:, :, :, lanes].astype(F32)
        source32[2] = source32[0] + source32[1]
        parts = [[] for _ in range(owners)]
        skewed = []
        for face in range(n_faces):
            if block == 0 and face % faces_each == 0:
                chunks[face // faces_each].wait()
            left_re = cond[0, face, :, lanes].astype(F32)
            left_im = cond[1, face, :, lanes].astype(F32)
            left_sum = left_re + left_im
            left_gap = left_im - left_re
            tiles = [None] * (2 * sources)
            for j in range(sources):
                both = jnp.sum((left_re * source32[2, j]).reshape(n_inner // 8, 8, LANES), 0)
                minus = jnp.sum((left_sum * source32[1, j]).reshape(n_inner // 8, 8, LANES), 0)
                plus = jnp.sum((left_gap * source32[0, j]).reshape(n_inner // 8, 8, LANES), 0)
                tiles[j] = both - minus
                tiles[sources + j] = both + plus
            first, size = groups[face]
            skewed.append(skew_block(sum_sublanes(tiles), face - first, CAP))
            if len(skewed) < size:
                continue
            moved = unskew_blocks(skewed, CAP)
            skewed = []
            for owner in range(owners):
                piece = moved[owner % size]
                if owner >= size:
                    piece = skew_block(piece, owners - owner // size * size, CAP)
                parts[owner].append(piece[:, : size * CAP])
        if block == 0:
            late[0].wait()
            spare = pack_coupling(coupling_out[0], 2 * sources)
        for owner in range(owners):
            out[place_of(block * owners + owner, out.shape[0])] = jnp.concatenate(parts[owner] + [spare], 1).astype(BF16)
    late[1].wait()


def assemble_kernel(received, place_rows, layer_rows, coupling, loads, out):
    peers, rows, _ = received.shape
    face_rows = place_rows.shape[1]
    layers, _, width = loads.shape
    place = iota((width, face_rows), 0)
    total = jnp.zeros((layers * rows, width), F32)
    whole_tiles = face_rows // LANES * LANES
    pieces = [(sender, at, LANES) for sender in range(peers) for at in range(0, whole_tiles, LANES)]
    pieces += [(sender, whole_tiles, face_rows - whole_tiles) for sender in range(peers) if face_rows > whole_tiles]
    place = iota((width, DEPTH), 0)
    while pieces:
        group = []
        while pieces and sum(piece[2] for piece in group) + pieces[0][2] <= DEPTH:
            group.append(pieces.pop(0))
        values, places, layer_row = [], [], []
        for sender, at, size in group:
            lanes = slice(at, at + size)
            values.append(received[place_of(sender, peers)].astype(F32)[:, lanes])
            places.append(place_rows[sender : sender + 1, :][:, lanes])
            layer_row.append(layer_rows[sender : sender + 1, :][:, lanes])
        values = jnp.concatenate(values, 1)
        layer_row = jnp.concatenate(layer_row, 1)
        onehot = jnp.where(place[:, : values.shape[1]] == jnp.concatenate(places, 1), 1.0, 0.0).astype(BF16)
        split = [jnp.where(layer_row == layer, values, 0.0) for layer in range(layers)]
        total += lax.dot_general(
            jnp.concatenate(split, 0).astype(BF16), onehot, (((1,), (1,)), ((), ())), preferred_element_type=F32
        )
    for layer in range(layers):
        loads[layer] = total[layer * rows : (layer + 1) * rows]
    block = couple(total[:rows], coupling[0], jnp.zeros((rows, width), F32)).astype(BF16)
    for peer in range(out.shape[0]):
        out[peer] = block


def couple(loads, coupling, carried):
    half = loads.shape[0] // 2
    couple_re, couple_im = coupling[0:1], coupling[1:2]
    real, imag = carried[:half], carried[half:]
    return jnp.concatenate(
        [
            loads[:half] - (couple_re * real - couple_im * imag),
            loads[half:] - (couple_re * imag + couple_im * real),
        ],
        0,
    )


def apply_schur(rhs, schur, layer):
    half = rhs.shape[0] // 2
    first = jnp.dot(rhs, schur[layer, 0], preferred_element_type=F32)
    second = jnp.dot(rhs, schur[layer, 1], preferred_element_type=F32)
    return jnp.concatenate([first[:half] - second[half:], second[:half] + first[half:]], 0)


def cross_kernel(everyone, whole, pairs, loads, coupling, schur, out, solved_out, row_out, *, row_axis):
    peers = whole.shape[0]
    _, count, width = loads.shape
    row = lax.axis_index(row_axis)
    row_out[0] = row
    start = jnp.maximum(row - 1, 0) * peers
    keep = (row > 0).astype(F32)
    blocks = []
    for peer in range(peers):
        place = place_of(peer, peers)
        before = everyone[start + peer].astype(F32) * keep
        blocks.append(couple(whole[place].astype(F32), pairs[peer], before).astype(BF16))
    solved = apply_schur(jnp.concatenate(blocks, 1), schur, 0)
    solved_out[...] = solved
    block = couple(loads[1], coupling[1], solved).astype(BF16)
    for peer in range(out.shape[0]):
        out[peer] = block


def side_by_side(gathered):
    count = gathered.shape[0]
    return jnp.concatenate([gathered[place_of(peer, count)] for peer in range(count)], 1)


def start_kernel(gathered, received, loads, coupling, schur, out, solved_out, row_out, pairs):
    row = lax.axis_index("sweep")
    row_out[0] = row
    layer_kernel(gathered, loads, coupling, schur, out, solved_out, layer=0)

    @pl.when(row == 0)
    def _():
        pairs[...] = jnp.zeros(pairs.shape, F32)

    @pl.when(row > 0)
    def _():
        peers, count, lanes = received.shape
        spare = lanes - 4 * pairs.shape[2] // count
        for peer in range(peers):
            pairs[peer] = unpack_coupling(received[place_of(peer, peers)].astype(F32)[:, spare:])


def layer_kernel(gathered, loads, coupling, schur, out, solved_out, *, layer):
    rhs = side_by_side(gathered)
    solved = apply_schur(rhs, schur, layer)
    solved_out[...] = solved
    block = couple(loads[layer + 1], coupling[layer + 1], solved).astype(BF16)
    for peer in range(out.shape[0]):
        out[peer] = block


def last_kernel(*refs, layer, send):
    gathered, *earlier, schur = refs[: layer + 2]
    outs = refs[layer + 2 :]
    rhs = side_by_side(gathered)
    solved = apply_schur(rhs, schur, layer)
    for at in range(layer):
        outs[0][at] = earlier[at][...]
    outs[0][layer] = solved
    if send:
        block = solved.astype(BF16)
        for peer in range(outs[1].shape[0]):
            outs[1][peer] = block


def call(kernel, out_shape, operands, scratch=(), space=pltpu.VMEM):
    if space == pltpu.HBM:
        operands = [pltpu.with_memory_space_constraint(operand, space) for operand in operands]
    return pl.pallas_call(
        kernel,
        out_shape=out_shape,
        in_specs=[pl.BlockSpec(memory_space=space)] * len(operands),
        out_specs=jax.tree.map(
            lambda out: pl.BlockSpec(memory_space=getattr(out, "memory_space", None) or pltpu.VMEM), out_shape
        ),
        scratch_shapes=list(scratch),
        compiler_params=pltpu.CompilerParams(vmem_limit_bytes=16 * 1024 * 1024),
    )(*operands)


def exchange_row(blocks):
    return lax.all_to_all(
        blocks, "xsec", split_axis=0, concat_axis=0, tiled=True,
        axis_index_groups=[row_order(blocks.shape[0])],
    )


def exchange_all(blocks):
    return lax.all_to_all(blocks, ("sweep", "xsec"), split_axis=0, concat_axis=0, tiled=True)


def shards(cond_block, interior_src, face_index, owner_count, coupling, schur_inv):
    layers = schur_inv.shape[0]
    width = schur_inv.shape[3]
    sources = interior_src.shape[3]
    n_faces, n_inner, elems = cond_block.shape[3:]
    peers = lax.axis_size("xsec")
    chain = lax.axis_size("sweep")
    count = 2 * sources
    struct = jax.ShapeDtypeStruct
    gathered_shape = struct((peers, count, width), BF16)

    index_rows = face_index[0, 0]
    outgoing, place_rows, layer_rows, coupling, schur_inv = call(
        contract_kernel,
        (
            struct((peers, count, n_faces * CAP + 4 * width // count), BF16),
            struct(index_rows.shape, index_rows.dtype),
            struct(index_rows.shape, index_rows.dtype),
            struct(coupling.shape, coupling.dtype),
            struct(schur_inv.shape, schur_inv.dtype),
        ),
        (cond_block[0, 0], interior_src[0, 0], index_rows, owner_count[0, 0], coupling, schur_inv),
        scratch=(
            pltpu.VMEM(cond_block.shape[2:], BF16),
            pltpu.VMEM(interior_src.shape[2:], BF16),
            pltpu.VMEM(index_rows.shape, index_rows.dtype),
            pltpu.SMEM(owner_count.shape[2:], owner_count.dtype),
            pltpu.VMEM((3, sources, n_inner, LANES), F32),
            pltpu.SemaphoreType.DMA((5 + CHUNKS,)),
        ),
        space=pltpu.HBM,
    )
    received = exchange_row(outgoing)
    loads, block = call(
        assemble_kernel,
        (struct((layers, count, width), F32), gathered_shape),
        (received, place_rows, layer_rows, coupling),
    )
    whole = exchange_row(block)
    solved_shape = struct((count, width), F32)
    whole_out = pltpu.VMEM((layers, count, width), F32)

    row_shape = pltpu.SMEM((1,), jnp.int32)

    def other_layers(block, solved, loads, coupling, schur_inv, send):
        done = [solved]
        for layer in range(1, layers - 1):
            block, solved = call(
                functools.partial(layer_kernel, layer=layer),
                (gathered_shape, solved_shape),
                (exchange_row(block), loads, coupling, schur_inv),
            )
            done.append(solved)
        sent = (struct((chain * peers, count, width), BF16),) if send else ()
        return call(
            functools.partial(last_kernel, layer=layers - 1, send=send),
            (whole_out,) + sent,
            (exchange_row(block), *done, schur_inv),
        )

    block, solved, row, pairs = call(
        start_kernel,
        (gathered_shape, solved_shape, row_shape, struct((peers, 2, width), F32)),
        (whole, received, loads, coupling, schur_inv),
    )
    finished = loads
    for round_at in range(chain):
        send = round_at < chain - 1
        nothing = struct((chain * peers, count, width), BF16)
        finished, *sent = lax.cond(
            row[0] == round_at,
            lambda finished, *rest: tuple(other_layers(*rest, send)),
            lambda finished, *rest: (finished,) + ((jnp.zeros(nothing.shape, BF16),) if send else ()),
            finished, block, solved, loads, coupling, schur_inv,
        )
        if send:
            block, solved, row = call(
                functools.partial(cross_kernel, row_axis="sweep"),
                (gathered_shape, solved_shape, row_shape),
                (exchange_all(sent[0]), whole, pairs, loads, coupling, schur_inv),
            )
    return finished


def solution(mesh):
    placed = (
        P("sweep", "xsec", None, None, None, None),
        P("sweep", "xsec", None, None, None, None),
        P("sweep", "xsec", None, None),
        P("sweep", "xsec", None),
        P("sweep", None, "xsec"),
        P("sweep", None, None, "xsec"),
    )
    return jax.shard_map(
        shards, mesh=mesh, in_specs=placed, out_specs=P("sweep", None, "xsec"), check_vma=False
    )
```
